256 devices in a mesh: tok: 8 (over y, core), lat: 32 (over x, z).
Axes of the slice: x: 4, y: 4, z: 8, core: 2. Of those that a mesh axis runs over, the one named last changes fastest.
Arguments:
- tokens: bfloat16 [2048, 8192], P(('tok', 'lat')), may hold values from -6 to 6
- enc_weight: bfloat16 [8192, 8192], P(None, 'lat'), may hold values from -0.0625 to 0.0625
- enc_bias: float32 [8192], P('lat'), may hold values from -3 to 3
- dec_weight: bfloat16 [8192, 8192], P('lat'), may hold values from -0.125 to 0.125
- dec_bias: float32 [8192], replicated, may hold values from -3 to 3
- active_blocks: int32 [16, 8], P('tok'), may hold values from 0 to 31, all different within a row
Outputs:
- reconstruction: bfloat16 [2048, 8192], P(('tok', 'lat'))
- enc_grad: float32 [8192, 8192], P('tok', 'lat')
- dec_grad: float32 [8192, 8192], P('lat', 'tok')
The draws below stay inside these ranges and needn't reach their ends.
Inputs may be any that keep to these rules, and one draw needn't show every extreme that they name: `active_blocks`: each row lists 8 different latent blocks, and every latent block is listed by some row.
All inputs are finite; a program needn't handle non-finite values.
Results may differ from the reference program's by a relative error of at most 0.013.
Values may be sent and summed in bfloat16 or wider, within the bound.
No kernel may reach another device: no remote copies, remote signals or barrier semaphores. Data moves between devices by JAX's collectives and lax.ppermute only.
A program may use at most 64 MiB of HBM per device.

```python
import math
import jax
import jax.numpy as jnp
from jax import lax

D = 8192
LB = 256
BLK = 128
BLK_DEV = 1
SLOTS = 8
GB = 2
NB = 32
LATENTS = 8192
TOKEN_BLOCKS = 16
TOKENS = 2048
GROUP = 256
N_LAT = 32


def block_scale(stream_key, extent, cuts, least, top_value):
    def one(axis_at, blocks):
        steps = jax.random.uniform(jax.random.fold_in(jax.random.fold_in(stream_key, 6), axis_at), (blocks,), jnp.float32, least / len(cuts), top_value / len(cuts))
        return jnp.repeat(jnp.exp(steps), extent[axis_at] // blocks).reshape((-1,) + (1,) * (len(extent) - axis_at - 1))

    level = one(*cuts[0])
    for cut in cuts[1:]:
        level = level * one(*cut)
    return level


def choose_distinct(stream_key, rows, count, top, lift):
    order = jax.random.permutation(jax.random.fold_in(stream_key, 1), count)
    pull = order
    for power in range(3):
        pull = pull * pull // count
    pull = pull * lift // count
    tickets = jax.random.randint(jax.random.fold_in(stream_key, 2), (rows, count), 0, 4096) + pull
    fixed_rows = jax.random.permutation(jax.random.fold_in(stream_key, 3), rows)[jnp.arange(count) % rows]
    tickets = jnp.where(jnp.arange(rows)[:, None] == fixed_rows[None, :], 1 << 14, tickets)
    priority = tickets * count + jnp.arange(count)
    return lax.top_k(priority.astype(jnp.int32), top)[1].astype(jnp.int32)


def noise(key, shape, scale, limit, cuts=(), kind=jnp.bfloat16):
    gain = block_scale(key, shape, cuts, -0.22, 0.18) if cuts else 1.0
    entries = jax.random.normal(key, shape, jnp.float32) * scale * gain
    return jnp.minimum(jnp.maximum(entries, -limit), limit).astype(kind)


def setup_inputs(seed: int = 0) -> dict:
    streams_of = jax.random.split(jax.random.key(seed), 7)
    tokens = noise(streams_of[0], (TOKENS, D), 1.0, 6.0, ((0, 256),))
    enc_weight = noise(streams_of[1], (D, LATENTS), D ** -0.5, 0.0625, ((1, 32),))
    enc_bias = noise(streams_of[2], (LATENTS,), 0.5, 3.0, ((0, 32),), jnp.float32)
    dec_weight = noise(streams_of[3], (LATENTS, D), (SLOTS * LB) ** -0.5, 0.125, ((0, 32),))
    dec_bias = noise(streams_of[4], (D,), 0.5, 3.0, (), jnp.float32)
    active_blocks = choose_distinct(streams_of[5], TOKEN_BLOCKS, NB, SLOTS, 4096)
    return dict(tokens=tokens, enc_weight=enc_weight, enc_bias=enc_bias, dec_weight=dec_weight, dec_bias=dec_bias, active_blocks=active_blocks)


def reference(tokens, enc_weight, enc_bias, dec_weight, dec_bias, active_blocks):
    latent_width = BLK_DEV * LB
    block_ids = jnp.arange(NB, dtype=jnp.int32)
    block_hits = jnp.any(active_blocks[:, :, None] == block_ids[None, None, :], axis=1).astype(jnp.float32)
    latent_gate = jnp.repeat(jnp.repeat(block_hits, LB, axis=1), BLK, axis=0)
    pre_act = jnp.dot(tokens, enc_weight, preferred_element_type=jnp.float32) + enc_bias.astype(jnp.float32)[None, :]
    activations = (jax.nn.silu(pre_act) * latent_gate).astype(jnp.bfloat16)

    def owner_term(running, owner_index):
        first_col = (owner_index * latent_width).astype(jnp.int32)
        owner_acts = lax.dynamic_slice_in_dim(activations, first_col, latent_width, 1)
        owner_rows = lax.dynamic_slice_in_dim(dec_weight, first_col, latent_width, 0)
        owner_part = jnp.dot(owner_acts, owner_rows, preferred_element_type=jnp.float32)
        owner_part = lax.optimization_barrier(owner_part.astype(jnp.bfloat16))
        return (running + owner_part.astype(jnp.float32), None)
    summed, _ = lax.scan(owner_term, jnp.zeros((TOKENS, D), jnp.float32), jnp.arange(N_LAT, dtype=jnp.int32))
    decoded = summed + dec_bias.astype(jnp.float32)[None, :]
    reconstruction = decoded.astype(jnp.bfloat16)
    cotangent = ((decoded - tokens.astype(jnp.float32)) * (1.0 / math.sqrt(TOKENS))).astype(jnp.bfloat16)
    latent_grad = jnp.dot(cotangent, dec_weight.T, preferred_element_type=jnp.float32)
    sigma = jax.nn.sigmoid(pre_act)
    pre_grad = (latent_grad * (sigma * (1.0 + pre_act * (1.0 - sigma))) * latent_gate).astype(jnp.bfloat16)

    def group_term(totals, group_index):
        enc_total, dec_total = totals
        first_row = (group_index * GROUP).astype(jnp.int32)
        group_tokens = lax.dynamic_slice_in_dim(tokens, first_row, GROUP, 0)
        group_grad = lax.dynamic_slice_in_dim(pre_grad, first_row, GROUP, 0)
        group_acts = lax.dynamic_slice_in_dim(activations, first_row, GROUP, 0)
        group_cot = lax.dynamic_slice_in_dim(cotangent, first_row, GROUP, 0)
        enc_part = jnp.dot(group_tokens.T, group_grad, preferred_element_type=jnp.float32)
        enc_part = lax.optimization_barrier(enc_part.astype(jnp.bfloat16))
        dec_part = jnp.dot(group_acts.T, group_cot, preferred_element_type=jnp.float32)
        dec_part = lax.optimization_barrier(dec_part.astype(jnp.bfloat16))
        return ((enc_total + enc_part.astype(jnp.float32), dec_total + dec_part.astype(jnp.float32)), None)
    start_totals = (jnp.zeros((D, LATENTS), jnp.float32), jnp.zeros((LATENTS, D), jnp.float32))
    totals, _ = lax.scan(group_term, start_totals, jnp.arange(TOKEN_BLOCKS // GB, dtype=jnp.int32))
    return (reconstruction, totals[0], totals[1])
```

```python
import math

import jax
import jax.numpy as jnp
from jax import lax
from jax.sharding import PartitionSpec as P

LB = 256
NX, NZ, NY, NC = 4, 8, 4, 2
BF = jnp.bfloat16
F32 = jnp.float32


def lat_shift(value, axis, step):
    if axis == "x":
        pairs = [(x * NZ + z, ((x + step) % NX) * NZ + z) for x in range(NX) for z in range(NZ)]
    else:
        pairs = [(x * NZ + z, x * NZ + (z + step) % NZ) for x in range(NX) for z in range(NZ)]
    return lax.ppermute(value, "lat", pairs)


def y_shift(value, step):
    pairs = [(y * NC + c, ((y + step) % NY) * NC + c) for y in range(NY) for c in range(NC)]
    return lax.ppermute(value, "tok", pairs)


def core_swap(value):
    pairs = [(y * NC + c, y * NC + 1 - c) for y in range(NY) for c in range(NC)]
    return lax.ppermute(value, "tok", pairs)


def ring_gather(block, axis, count):
    far = count // 2
    half = block.shape[0] // 2
    found = [None] * count
    found[0] = up = down = block
    for k in range(1, far):
        found[k] = up = lat_shift(up, axis, -1)
        found[count - k] = down = lat_shift(down, axis, 1)
    found[far] = jnp.concatenate(
        [lat_shift(up[:half], axis, -1), lat_shift(down[half:], axis, 1)], axis=0
    )
    return found


def add(left, right):
    return (left.astype(F32) + right.astype(F32)).astype(BF)


def ring_sum(terms, axis, count):
    far = count // 2
    half = terms[0].shape[0] // 2
    up = lat_shift(terms[far][:half], axis, 1)
    down = lat_shift(terms[far][half:], axis, -1)
    for k in range(far - 1, 0, -1):
        if k == far - 1:
            head, tail = terms[k][:half], terms[k][half:]
            up = jnp.concatenate([add(head, up), tail], axis=0)
            head, tail = terms[count - k][:half], terms[count - k][half:]
            down = jnp.concatenate([head, add(tail, down)], axis=0)
        else:
            up = add(terms[k], up)
            down = add(terms[count - k], down)
        up = lat_shift(up, axis, 1)
        down = lat_shift(down, axis, -1)
    return terms[0].astype(F32) + up.astype(F32) + down.astype(F32)


def gather_lat(block, x_first):
    rows, width = block.shape
    if x_first:
        line = jnp.stack(ring_gather(block, "x", NX), axis=0)
        whole = jnp.stack(ring_gather(line, "z", NZ), axis=1)
    else:
        line = jnp.stack(ring_gather(block, "z", NZ), axis=0)
        whole = jnp.stack(ring_gather(line, "x", NX), axis=0)
    return whole.reshape(NX * NZ * rows, width)


def sum_lat(whole, z_first):
    width = whole.shape[1]
    whole = whole.reshape(NX, NZ, -1, width)
    if z_first:
        line = ring_sum([whole[:, k] for k in range(NZ)], "z", NZ).astype(BF)
        return ring_sum([line[k] for k in range(NX)], "x", NX)
    line = ring_sum([whole[k] for k in range(NX)], "x", NX).astype(BF)
    return ring_sum([line[k] for k in range(NZ)], "z", NZ)


def sum_y(parts):
    y_here = lax.axis_index("tok") // NC
    sent = parts.astype(BF)
    total = lax.dynamic_index_in_dim(sent, y_here, 0, keepdims=False).astype(F32)
    for k in range(1, NY):
        piece = lax.dynamic_index_in_dim(sent, (y_here + k) % NY, 0, keepdims=False)
        total = total + y_shift(piece, k).astype(F32)
    return total


def shards(tokens, enc_weight, enc_bias, dec_weight, dec_bias, active_blocks):
    rows, depth = tokens.shape
    latent_width = enc_weight.shape[1]
    lat_count = NX * NZ
    part = depth // (NY * NC * 2)
    cot_scale = 1.0 / math.sqrt(rows * lat_count * NY * NC)
    owner = lax.axis_index("lat")
    core = lax.axis_index("tok") % NC
    x_here = owner // NZ

    tok_cols = tokens.reshape(rows, NY, NC, 2, part)
    mine = lax.dynamic_index_in_dim(tok_cols, core, 2, keepdims=False)
    other = lax.dynamic_index_in_dim(tok_cols, 1 - core, 2, keepdims=False)
    came = core_swap(other)
    own = [
        jnp.concatenate(
            [mine[:, :, h].reshape(rows, NY * part), came[:, :, h].reshape(rows, NY * part)],
            axis=0,
        )
        for h in range(2)
    ]
    enc_cols = lax.dynamic_index_in_dim(
        enc_weight.reshape(NY, NC, 2, part, latent_width), core, 1, keepdims=False
    )
    enc_w = [enc_cols[:, h].reshape(NY * part, latent_width) for h in range(2)]
    dec_cols = lax.dynamic_index_in_dim(
        dec_weight.reshape(latent_width, NY, NC, 2, part), core, 2, keepdims=False
    )
    dec_w = [dec_cols[:, :, h].reshape(latent_width, NY * part) for h in range(2)]
    bias_cols = lax.dynamic_index_in_dim(
        dec_bias.reshape(NY, NC, 2, part), core, 1, keepdims=False
    )
    bias_d = [bias_cols[:, h].reshape(1, NY * part) for h in range(2)]

    hits = jnp.any(active_blocks == owner, axis=1).astype(F32)
    x_owner = (x_here + jnp.arange(NX)) % NX
    blocks_x = NX // active_blocks.shape[0]
    gate = sum(
        jnp.where(x_owner // blocks_x == b, hits[b], 0.0) for b in range(active_blocks.shape[0])
    )
    gate = jnp.repeat(gate, NZ)[:, None, None]

    gathered = [gather_lat(own[0], True), gather_lat(own[1], False)]
    partial = (
        jnp.dot(gathered[0], enc_w[0], preferred_element_type=F32)
        + jnp.dot(gathered[1], enc_w[1], preferred_element_type=F32)
    ).reshape(lat_count, 2, rows, latent_width)
    pre_act = partial[:, 0] + core_swap(partial[:, 1]) + enc_bias[None, None, :]
    act = (jax.nn.silu(pre_act) * gate).astype(BF)
    sigma = jax.nn.sigmoid(pre_act)
    slope = sigma * (1.0 + pre_act * (1.0 - sigma)) * gate
    acts = jnp.stack([act, core_swap(act)], axis=1).reshape(-1, latent_width)

    cot_own, recon = [], []
    for h in range(2):
        term = jnp.dot(acts, dec_w[h], preferred_element_type=F32).astype(BF)
        decoded = sum_lat(term, h == 0) + bias_d[h]
        recon.append(decoded.astype(BF).reshape(2, rows, NY, part))
        cot_own.append(((decoded - own[h].astype(F32)) * cot_scale).astype(BF))
    cot = [gather_lat(cot_own[0], True), gather_lat(cot_own[1], False)]

    recon_all = jnp.stack(recon, axis=3)
    recon_mine = recon_all[0]
    recon_came = core_swap(recon_all[1])
    first = jnp.where(core == 0, recon_mine, recon_came)
    second = jnp.where(core == 0, recon_came, recon_mine)
    reconstruction = jnp.stack([first, second], axis=2).reshape(rows, depth)

    over_cols = (((1,), (1,)), ((), ()))
    over_rows = (((0,), (0,)), ((), ()))
    grad = (
        lax.dot_general(cot[0], dec_w[0], over_cols, preferred_element_type=F32)
        + lax.dot_general(cot[1], dec_w[1], over_cols, preferred_element_type=F32)
    ).reshape(lat_count, 2, rows, latent_width)
    pre_grad = ((grad[:, 0] + core_swap(grad[:, 1])) * slope).astype(BF)
    pre_grads = jnp.stack([pre_grad, core_swap(pre_grad)], axis=1).reshape(-1, latent_width)

    dec_parts, enc_parts = [], []
    for h in range(2):
        dec_part = lax.dot_general(acts, cot[h], over_rows, preferred_element_type=F32)
        dec_parts.append(
            sum_y(jnp.swapaxes(dec_part.reshape(latent_width, NY, part), 0, 1))
        )
    for h in range(2):
        enc_part = lax.dot_general(
            gathered[h], pre_grads, over_rows, preferred_element_type=F32
        )
        enc_parts.append(sum_y(enc_part.reshape(NY, part, latent_width)))
    return (
        reconstruction,
        jnp.concatenate(enc_parts, axis=0),
        jnp.concatenate(dec_parts, axis=1),
    )


def solution(mesh):
    placed = (
        P(("tok", "lat"), None),
        P(None, "lat"),
        P("lat"),
        P("lat", None),
        P(),
        P("tok", None),
    )
    return jax.shard_map(
        shards,
        mesh=mesh,
        in_specs=placed,
        out_specs=(P(("tok", "lat"), None), P("tok", "lat"), P("lat", "tok")),
        check_vma=False,
    )
```

```python
import math

import jax
import jax.numpy as jnp
from jax import lax
from jax.sharding import PartitionSpec as P

LB = 256
NX, NZ, NY, NC = 4, 8, 4, 2
NS = NZ // 2
BF = jnp.bfloat16
F32 = jnp.float32
BOTH = ("tok", "lat")


def index_of(y, c, x, z):
    return (((y % NY) * NC + c) * NX + x % NX) * NZ + z % NZ


def everywhere(cores=(0, 1)):
    return [
        (y, c, x, z) for y in range(NY) for c in cores for x in range(NX) for z in range(NZ)
    ]


def x_shift(value, step):
    pairs = [(index_of(y, c, x, z), index_of(y, c, x + step, z)) for y, c, x, z in everywhere()]
    return lax.ppermute(value, BOTH, pairs)


def y_shift(value, step):
    pairs = [(index_of(y, c, x, z), index_of(y + step, c, x, z)) for y, c, x, z in everywhere()]
    return lax.ppermute(value, BOTH, pairs)


def z_turn(value, step, cores=(0, 1)):
    pairs = [
        (index_of(y, c, x, z), index_of(y, c, x, z + (step if c == 0 else -step)))
        for y, c, x, z in everywhere(cores)
    ]
    return lax.ppermute(value, BOTH, pairs)


def core_swap(value):
    pairs = [(index_of(y, c, x, z), index_of(y, 1 - c, x, z)) for y, c, x, z in everywhere()]
    return lax.ppermute(value, BOTH, pairs)


def add(left, right):
    return (left.astype(F32) + right.astype(F32)).astype(BF)


def gather_x(block):
    return [block] + [x_shift(block, -k) for k in range(1, NX)]


def gather_z(block, core):
    found = [block]
    for _ in range(NS - 1):
        found.append(z_turn(found[-1], -1))
    last = z_turn(found[-1], -1, cores=(1,))
    return [jnp.where(core == 0, block, last)] + found[1:]


def sum_x(terms):
    came = [x_shift(terms[k], k) for k in range(1, NX)]
    total = terms[0].astype(F32)
    for piece in came:
        total = total + piece.astype(F32)
    return total


def sum_z(terms, core):
    running = z_turn(terms[0], 1, cores=(1,))
    for k in range(NS - 1, 0, -1):
        running = z_turn(add(terms[k], running), 1)
    return running.astype(F32) + jnp.where(core == 0, terms[0].astype(F32), 0.0)


def gather_a(own, core):
    line = jnp.stack(gather_x(own), axis=0)
    chip = jnp.stack([line, core_swap(line)], axis=1)
    return jnp.stack(gather_z(chip, core), axis=0)


def gather_b(own, core):
    chip = jnp.stack([own, core_swap(own)], axis=0)
    side = jnp.stack(gather_z(chip, core), axis=0)
    return jnp.stack(gather_x(side), axis=1)


def scatter_a(terms, core):
    side = sum_z([terms[s] for s in range(NS)], core)
    line = (side[:, 0] + core_swap(side[:, 1].astype(BF)).astype(F32)).astype(BF)
    return sum_x([line[k] for k in range(NX)])


def scatter_b(terms, core):
    side = sum_x([terms[:, k] for k in range(NX)]).astype(BF)
    chip = sum_z([side[s] for s in range(NS)], core)
    return chip[0] + core_swap(chip[1].astype(BF)).astype(F32)


def sum_tok(whole, core):
    rows, depth = whole.shape
    part = depth // (NY * NC)
    y_here = lax.axis_index("tok") // NC

    def take(first, c):
        return lax.dynamic_slice_in_dim(whole, ((first % NY) * NC + c) * part, part, 1)

    mine = jnp.concatenate([take(y_here + k, core) for k in range(NY)], axis=0)
    other = jnp.concatenate([take(y_here + k, 1 - core) for k in range(NY)], axis=0)
    chip = (mine.astype(F32) + core_swap(other).astype(F32)).reshape(NY, rows, part)
    total = chip[0]
    for k in range(1, NY):
        total = total + y_shift(chip[k].astype(BF), k).astype(F32)
    return total


def shards(tokens, enc_weight, enc_bias, dec_weight, dec_bias, active_blocks):
    rows, depth = tokens.shape
    latent_width = enc_weight.shape[1]
    half = depth // 2
    here = NS * NX * NC * rows
    cot_scale = 1.0 / math.sqrt(rows * NX * NZ * NY * NC)
    owner = lax.axis_index("lat")
    core = lax.axis_index("tok") % NC
    x_here = owner // NZ

    lists = jnp.stack([active_blocks, core_swap(active_blocks)], axis=0)
    hits = jnp.any(lists == owner, axis=2).astype(F32)
    blocks = active_blocks.shape[0]
    x_block = ((x_here + jnp.arange(NX)) % NX) // (NX // blocks)
    gate = sum(jnp.where(x_block[:, None] == b, hits[None, :, b], 0.0) for b in range(blocks))
    gate = jnp.broadcast_to(gate[None, :, :, None], (NS, NX, NC, rows)).reshape(here, 1)

    def gather(own):
        parts = [gather_a(own[:, :half], core), gather_b(own[:, half:], core)]
        return jnp.concatenate([p.reshape(here, half) for p in parts], axis=1)

    gathered = gather(tokens)
    pre_act = jnp.dot(gathered, enc_weight, preferred_element_type=F32) + enc_bias[None, :]
    act = (jax.nn.silu(pre_act) * gate).astype(BF)
    sigma = jax.nn.sigmoid(pre_act)
    slope = sigma * (1.0 + pre_act * (1.0 - sigma)) * gate

    term = jnp.dot(act, dec_weight, preferred_element_type=F32).astype(BF)
    shape = (NS, NX, NC, rows, half)
    decoded = jnp.concatenate(
        [
            scatter_a(term[:, :half].reshape(shape), core),
            scatter_b(term[:, half:].reshape(shape), core),
        ],
        axis=1,
    ) + dec_bias[None, :]
    cot_own = ((decoded - tokens.astype(F32)) * cot_scale).astype(BF)
    cot = gather(cot_own)

    over_cols = (((1,), (1,)), ((), ()))
    over_rows = (((0,), (0,)), ((), ()))
    grad = lax.dot_general(cot, dec_weight, over_cols, preferred_element_type=F32)
    pre_grad = (grad * slope).astype(BF)
    dec_part = lax.dot_general(act, cot, over_rows, preferred_element_type=F32).astype(BF)
    enc_part = lax.dot_general(
        pre_grad, gathered, over_rows, preferred_element_type=F32
    ).astype(BF)
    dec_grad = sum_tok(dec_part, core)
    enc_grad = sum_tok(enc_part, core).T
    return (decoded.astype(BF), enc_grad, dec_grad)


def solution(mesh):
    placed = (
        P(("tok", "lat"), None),
        P(None, "lat"),
        P("lat"),
        P("lat", None),
        P(),
        P("tok", None),
    )
    return jax.shard_map(
        shards,
        mesh=mesh,
        in_specs=placed,
        out_specs=(P(("tok", "lat"), None), P("tok", "lat"), P("lat", "tok")),
        check_vma=False,
    )
```

```python
import math

import jax
import jax.numpy as jnp
from jax import lax
from jax.sharding import PartitionSpec as P

LB = 256
NX, NZ, NY, NC = 4, 8, 4, 2
NS = NZ // 2
BF = jnp.bfloat16
F32 = jnp.float32
BOTH = ("tok", "lat")


def index_of(y, c, x, z):
    return (((y % NY) * NC + c) * NX + x % NX) * NZ + z % NZ


def everywhere(cores=(0, 1)):
    return [
        (y, c, x, z) for y in range(NY) for c in cores for x in range(NX) for z in range(NZ)
    ]


def x_shift(value, step):
    pairs = [(index_of(y, c, x, z), index_of(y, c, x + step, z)) for y, c, x, z in everywhere()]
    return lax.ppermute(value, BOTH, pairs)


def y_shift(value, step):
    pairs = [(index_of(y, c, x, z), index_of(y + step, c, x, z)) for y, c, x, z in everywhere()]
    return lax.ppermute(value, BOTH, pairs)


def z_turn(value, step, cores=(0, 1)):
    pairs = [
        (index_of(y, c, x, z), index_of(y, c, x, z + (step if c == 0 else -step)))
        for y, c, x, z in everywhere(cores)
    ]
    return lax.ppermute(value, BOTH, pairs)


def core_swap(value):
    pairs = [(index_of(y, c, x, z), index_of(y, 1 - c, x, z)) for y, c, x, z in everywhere()]
    return lax.ppermute(value, BOTH, pairs)


def add(left, right):
    return (left.astype(F32) + right.astype(F32)).astype(BF)


def tie(*values):
    return lax.optimization_barrier(values)


def gather(own_a, own_b, core, extra):
    first = core == 0
    width = own_a.shape[1]
    chip_b = jnp.stack([own_b, core_swap(own_b)], axis=0)
    line = jnp.stack([own_a] + [x_shift(own_a, -k) for k in range(1, NX)], axis=0)
    one, two = z_turn(chip_b, -1), z_turn(chip_b, -2)
    chip_a = jnp.stack([line, core_swap(line)], axis=1)
    step_1 = z_turn(chip_a, -1)
    far = z_turn(jnp.stack([one, two], axis=0), -2)
    side = jnp.stack([jnp.where(first, chip_b, far[1]), one, two, far[0]], axis=0)
    side, step_1, extra = tie(side, step_1, extra)
    next_x, last_x = x_shift(side, -1), x_shift(side, 1)
    step_2 = z_turn(step_1, -1)
    next_x, last_x, step_2 = tie(next_x, last_x, step_2)
    half = NS // 2
    far_x = jnp.concatenate([x_shift(next_x[:half], -1), x_shift(last_x[half:], 1)], axis=0)
    step_3 = z_turn(step_2, -1)
    step_4 = z_turn(step_3, -1, cores=(1,))
    whole_b = jnp.stack([side, next_x, far_x, last_x], axis=0)
    whole_a = jnp.stack([jnp.where(first, chip_a, step_4), step_1, step_2, step_3], axis=0)
    return whole_a.reshape(-1, width), whole_b.reshape(-1, width), extra


def scatter(terms_a, terms_b, core):
    first = core == 0
    half = NS // 2
    up = x_shift(jnp.stack([terms_b[2, :half], terms_b[1, half:]], axis=0), 1)
    down = x_shift(jnp.stack([terms_b[3, :half], terms_b[2, half:]], axis=0), -1)
    step = z_turn(terms_a[0], 1, cores=(1,))
    up, down, step = tie(up, down, step)
    up_last = x_shift(add(terms_b[1, :half], up[0]), 1)
    down_last = x_shift(add(terms_b[3, half:], down[1]), -1)
    step = z_turn(add(terms_a[3], step), 1)
    up_last, down_last, step = tie(up_last, down_last, step)
    head = terms_b[0, :half].astype(F32) + up_last.astype(F32) + down[0].astype(F32)
    tail = terms_b[0, half:].astype(F32) + down_last.astype(F32) + up[1].astype(F32)
    far = z_turn(jnp.stack([tail[-1].astype(BF), head[0].astype(BF)], axis=0), 2)
    step = z_turn(add(terms_a[2], step), 1)
    far, step = tie(far, step)
    one = z_turn(add(head[1], far[0]), 1)
    two = z_turn(add(tail[0], jnp.where(first, jnp.zeros_like(far[1]), far[1])), 2)
    step = z_turn(add(terms_a[1], step), 1)
    one, two, step = tie(one, two, step)

    chip_a = step.astype(F32) + jnp.where(first, terms_a[0].astype(F32), 0.0)
    chip_b = one.astype(F32) + two.astype(F32) + jnp.where(first, head[0], 0.0)
    line = (chip_a[:, 0] + core_swap(chip_a[:, 1].astype(BF)).astype(F32)).astype(BF)
    total_b = chip_b[0] + core_swap(chip_b[1].astype(BF)).astype(F32)
    total_a = line[0].astype(F32)
    for piece in [x_shift(line[k], k) for k in range(1, NX)]:
        total_a = total_a + piece.astype(F32)
    return total_a, total_b


def split_tok(whole, core):
    part = whole.shape[1] // (NY * NC)
    y_here = lax.axis_index("tok") // NC

    def take(first, c):
        return lax.dynamic_slice_in_dim(whole, ((first % NY) * NC + c) * part, part, 1)

    return [
        jnp.stack([take(y_here + k, c) for k in range(NY)], axis=0) for c in (core, 1 - core)
    ]


def y_first(chip):
    half = chip.shape[1] // 2
    up = y_shift(jnp.stack([chip[2, :half], chip[1, half:]], axis=0), 1)
    down = y_shift(jnp.stack([chip[3, :half], chip[2, half:]], axis=0), -1)
    return up, down


def y_second(chip, up, down):
    half = chip.shape[1] // 2
    up_last = y_shift(add(chip[1, :half], up[0]), 1)
    down_last = y_shift(add(chip[3, half:], down[1]), -1)
    return up_last, down_last


def y_total(chip, up, down, up_last, down_last):
    half = chip.shape[1] // 2
    head = chip[0, :half].astype(F32) + up_last.astype(F32) + down[0].astype(F32)
    tail = chip[0, half:].astype(F32) + down_last.astype(F32) + up[1].astype(F32)
    return jnp.concatenate([head, tail], axis=0)


def shards(tokens, enc_weight, enc_bias, dec_weight, dec_bias, active_blocks):
    rows, depth = tokens.shape
    latent_width = enc_weight.shape[1]
    half = depth // 2
    here = NS * NX * NC * rows
    cot_scale = 1.0 / math.sqrt(rows * NX * NZ * NY * NC)
    owner = lax.axis_index("lat")
    core = lax.axis_index("tok") % NC
    x_here = owner // NZ

    def swapped(rows_b, outer, inner):
        shaped = rows_b.reshape(outer, inner, NC * rows, -1)
        return jnp.swapaxes(shaped, 0, 1).reshape(here, -1)

    tok_a, tok_b, lists = gather(tokens[:, :half], tokens[:, half:], core, active_blocks)

    lists = jnp.stack([lists, core_swap(lists)], axis=0)
    hits = jnp.any(lists == owner, axis=2).astype(F32)
    blocks = active_blocks.shape[0]
    x_block = ((x_here + jnp.arange(NX)) % NX) // (NX // blocks)
    gate = sum(jnp.where(x_block[:, None] == b, hits[None, :, b], 0.0) for b in range(blocks))
    gate = jnp.broadcast_to(gate[None, :, :, None], (NS, NX, NC, rows)).reshape(here, 1)

    pre_b = jnp.dot(tok_b, enc_weight[half:], preferred_element_type=F32)
    pre_act = jnp.dot(tok_a, enc_weight[:half], preferred_element_type=F32)
    pre_act = pre_act + swapped(pre_b, NX, NS) + enc_bias[None, :]
    act = (jax.nn.silu(pre_act) * gate).astype(BF)
    act_b = swapped(act, NS, NX)
    sigma = jax.nn.sigmoid(pre_act)
    slope = sigma * (1.0 + pre_act * (1.0 - sigma)) * gate
    act, act_b, slope = tie(act, act_b, slope)

    term_b = jnp.dot(act_b, dec_weight[:, half:], preferred_element_type=F32).astype(BF)
    term_a = jnp.dot(act, dec_weight[:, :half], preferred_element_type=F32).astype(BF)
    decoded = scatter(
        term_a.reshape(NS, NX, NC, rows, half), term_b.reshape(NX, NS, NC, rows, half), core
    )
    recon, cot_own = [], []
    for h, total in enumerate(decoded):
        cols = slice(h * half, (h + 1) * half)
        total = total + dec_bias[None, cols]
        recon.append(total.astype(BF))
        cot_own.append(((total - tokens[:, cols].astype(F32)) * cot_scale).astype(BF))
    cot_a, cot_b, slope = gather(cot_own[0], cot_own[1], core, slope)

    over_cols = (((1,), (1,)), ((), ()))
    over_rows = (((0,), (0,)), ((), ()))

    def product(left, right, dims):
        return lax.dot_general(left, right, dims, preferred_element_type=F32)

    dec_part = jnp.concatenate(
        [product(act, cot_a, over_rows).astype(BF), product(act_b, cot_b, over_rows).astype(BF)],
        axis=1,
    )
    dec_mine, dec_other = split_tok(dec_part, core)
    dec_mine, dec_other, cot_a, cot_b = tie(dec_mine, dec_other, cot_a, cot_b)
    dec_came = core_swap(dec_other)
    grad = product(cot_a, dec_weight[:, :half], over_cols) + swapped(
        product(cot_b, dec_weight[:, half:], over_cols), NX, NS
    )
    pre_grad = (grad * slope).astype(BF)
    pre_grad, pre_grad_b, dec_came = tie(pre_grad, swapped(pre_grad, NS, NX), dec_came)
    dec_chip = add(dec_mine, dec_came)
    dec_up, dec_down = y_first(dec_chip)
    enc_part = jnp.concatenate(
        [product(pre_grad, tok_a, over_rows).astype(BF), product(pre_grad_b, tok_b, over_rows).astype(BF)],
        axis=1,
    )
    enc_mine, enc_other = split_tok(enc_part, core)
    enc_chip = add(enc_mine, core_swap(enc_other))
    dec_up, dec_down, enc_chip = tie(dec_up, dec_down, enc_chip)
    enc_up, enc_down = y_first(enc_chip)
    dec_last = y_second(dec_chip, dec_up, dec_down)
    enc_up, enc_down, dec_last = tie(enc_up, enc_down, dec_last)
    enc_last = y_second(enc_chip, enc_up, enc_down)
    dec_grad = y_total(dec_chip, dec_up, dec_down, *dec_last)
    enc_grad = y_total(enc_chip, enc_up, enc_down, *enc_last).T
    return (jnp.concatenate(recon, axis=1), enc_grad, dec_grad)


def solution(mesh):
    placed = (
        P(("tok", "lat"), None),
        P(None, "lat"),
        P("lat"),
        P("lat", None),
        P(),
        P("tok", None),
    )
    return jax.shard_map(
        shards,
        mesh=mesh,
        in_specs=placed,
        out_specs=(P(("tok", "lat"), None), P("tok", "lat"), P("lat", "tok")),
        check_vma=False,
    )
```

```python
import math

import jax
import jax.numpy as jnp
from jax import lax
from jax.sharding import PartitionSpec as P

LB = 256
NX, NZ, NY, NC = 4, 8, 4, 2
NS = NZ // 2
BF = jnp.bfloat16
F32 = jnp.float32
BOTH = ("tok", "lat")


def index_of(y, c, x, z):
    return (((y % NY) * NC + c) * NX + x % NX) * NZ + z % NZ


def everywhere(cores=(0, 1)):
    return [
        (y, c, x, z) for y in range(NY) for c in cores for x in range(NX) for z in range(NZ)
    ]


def x_shift(value, step):
    pairs = [(index_of(y, c, x, z), index_of(y, c, x + step, z)) for y, c, x, z in everywhere()]
    return lax.ppermute(value, BOTH, pairs)


def y_shift(value, step):
    pairs = [(index_of(y, c, x, z), index_of(y + step, c, x, z)) for y, c, x, z in everywhere()]
    return lax.ppermute(value, BOTH, pairs)


def z_turn(value, step, cores=(0, 1)):
    pairs = [
        (index_of(y, c, x, z), index_of(y, c, x, z + (step if c == 0 else -step)))
        for y, c, x, z in everywhere(cores)
    ]
    return lax.ppermute(value, BOTH, pairs)


def core_swap(value):
    pairs = [(index_of(y, c, x, z), index_of(y, 1 - c, x, z)) for y, c, x, z in everywhere()]
    return lax.ppermute(value, BOTH, pairs)


def add(left, right):
    return (left.astype(F32) + right.astype(F32)).astype(BF)


def tie(*values):
    return lax.optimization_barrier(values)


def gather(own_a, own_b, core, extra):
    first = core == 0
    width = own_a.shape[1]
    chip_b = jnp.stack([own_b, core_swap(own_b)], axis=0)
    line = jnp.stack([own_a] + [x_shift(own_a, -k) for k in range(1, NX)], axis=0)
    one, two = z_turn(chip_b, -1), z_turn(chip_b, -2)
    chip_a = jnp.stack([line, core_swap(line)], axis=1)
    step_1 = z_turn(chip_a, -1)
    near = jnp.stack([one, two], axis=0)
    far = z_turn(near, -2)
    near_1, near_3 = x_shift(near, -1), x_shift(near, 1)
    ends = jnp.stack([jnp.where(first, chip_b, far[1]), far[0]], axis=0)
    ends, step_1, near_1, near_3, extra = tie(ends, step_1, near_1, near_3, extra)
    ends_1, ends_3 = x_shift(ends, -1), x_shift(ends, 1)
    step_2 = z_turn(step_1, -1)
    ends_1, ends_3, step_2 = tie(ends_1, ends_3, step_2)
    near_2, ends_2 = x_shift(near_1, -1), x_shift(ends_3, 1)
    step_3 = z_turn(step_2, -1)
    step_4 = z_turn(step_3, -1, cores=(1,))
    whole_b = jnp.stack([ends, near, ends_1, near_1, ends_2, near_2, ends_3, near_3], axis=0)
    whole_a = jnp.stack([jnp.where(first, chip_a, step_4), step_3, step_1, step_2], axis=0)
    return whole_a.reshape(-1, width), whole_b.reshape(-1, width), extra


def scatter(terms_a, terms_b, core):
    first = core == 0
    ends = [terms_b[k, :2] for k in range(NX)]
    near = [terms_b[k, 2:] for k in range(NX)]
    ends_up, ends_far = x_shift(ends[1], 1), x_shift(ends[2], -1)
    step = z_turn(terms_a[0], 1, cores=(1,))
    ends_up, ends_far, step = tie(ends_up, ends_far, step)
    ends_down = x_shift(add(ends[3], ends_far), -1)
    near_far = x_shift(near[2], 1)
    step = z_turn(add(terms_a[1], step), 1)
    ends_down, near_far, step = tie(ends_down, near_far, step)
    ends_sum = (ends[0].astype(F32) + ends_up.astype(F32) + ends_down.astype(F32)).astype(BF)
    far = z_turn(ends_sum, 2)
    near_up, near_down = x_shift(add(near[1], near_far), 1), x_shift(near[3], -1)
    step = z_turn(add(terms_a[3], step), 1)
    far, near_up, near_down, step = tie(far, near_up, near_down, step)
    near_sum = near[0].astype(F32) + near_up.astype(F32) + near_down.astype(F32)
    one = z_turn(add(near_sum[0], far[1]), 1)
    two = z_turn(add(near_sum[1], jnp.where(first, jnp.zeros_like(far[0]), far[0])), 2)
    step = z_turn(add(terms_a[2], step), 1)

    chip_a = step.astype(F32) + jnp.where(first, terms_a[0].astype(F32), 0.0)
    chip_b = one.astype(F32) + two.astype(F32) + jnp.where(first, ends_sum[0].astype(F32), 0.0)
    line = (chip_a[:, 0] + core_swap(chip_a[:, 1].astype(BF)).astype(F32)).astype(BF)
    total_b = chip_b[0] + core_swap(chip_b[1].astype(BF)).astype(F32)
    total_a = line[0].astype(F32)
    for piece in [x_shift(line[k], k) for k in range(1, NX)]:
        total_a = total_a + piece.astype(F32)
    return total_a, total_b


def split_core(part, core):
    blocks = NY // 2
    block = part.shape[1] // (blocks * NC)

    def take(c):
        pieces = [
            lax.dynamic_slice_in_dim(part, (j * NC + c) * block, block, 1) for j in range(blocks)
        ]
        return jnp.stack(pieces, axis=0)

    return take(core), take(1 - core)


def from_here(low, high):
    whole = jnp.concatenate([low, high], axis=0)
    y_here = lax.axis_index("tok") // NC
    return jnp.stack(
        [lax.dynamic_index_in_dim(whole, (y_here + k) % NY, 0, keepdims=False) for k in range(NY)],
        axis=0,
    )


def y_first(chip):
    half = chip.shape[1] // 2
    up = y_shift(jnp.stack([chip[2, :half], chip[1, half:]], axis=0), 1)
    down = y_shift(jnp.stack([chip[3, :half], chip[2, half:]], axis=0), -1)
    return up, down


def y_second(chip, up, down):
    half = chip.shape[1] // 2
    up_last = y_shift(add(chip[1, :half], up[0]), 1)
    down_last = y_shift(add(chip[3, half:], down[1]), -1)
    return up_last, down_last


def y_total(chip, up, down, up_last, down_last):
    half = chip.shape[1] // 2
    head = chip[0, :half].astype(F32) + up_last.astype(F32) + down[0].astype(F32)
    tail = chip[0, half:].astype(F32) + down_last.astype(F32) + up[1].astype(F32)
    return jnp.concatenate([head, tail], axis=0)


def shards(tokens, enc_weight, enc_bias, dec_weight, dec_bias, active_blocks):
    rows, depth = tokens.shape
    latent_width = enc_weight.shape[1]
    half = depth // 2
    here = NS * NX * NC * rows
    cot_scale = 1.0 / math.sqrt(rows * NX * NZ * NY * NC)
    owner = lax.axis_index("lat")
    core = lax.axis_index("tok") % NC
    x_here = owner // NZ

    def swapped(rows_b, outer, inner):
        shaped = rows_b.reshape(outer, inner, NC * rows, -1)
        return jnp.swapaxes(shaped, 0, 1).reshape(here, -1)

    tok_a, tok_b, lists = gather(tokens[:, :half], tokens[:, half:], core, active_blocks)

    lists = jnp.stack([lists, core_swap(lists)], axis=0)
    hits = jnp.any(lists == owner, axis=2).astype(F32)
    blocks = active_blocks.shape[0]
    x_block = ((x_here + jnp.arange(NX)) % NX) // (NX // blocks)
    gate = sum(jnp.where(x_block[:, None] == b, hits[None, :, b], 0.0) for b in range(blocks))
    gate = jnp.broadcast_to(gate[None, :, :, None], (NS, NX, NC, rows)).reshape(here, 1)

    pre_b = jnp.dot(tok_b, enc_weight[half:], preferred_element_type=F32)
    pre_act = jnp.dot(tok_a, enc_weight[:half], preferred_element_type=F32)
    pre_act = pre_act + swapped(pre_b, NX, NS) + enc_bias[None, :]
    act = (jax.nn.silu(pre_act) * gate).astype(BF)
    act_b = swapped(act, NS, NX)
    sigma = jax.nn.sigmoid(pre_act)
    slope = sigma * (1.0 + pre_act * (1.0 - sigma)) * gate
    act, act_b, slope = tie(act, act_b, slope)

    term_b = jnp.dot(act_b, dec_weight[:, half:], preferred_element_type=F32).astype(BF)
    term_a = jnp.dot(act, dec_weight[:, :half], preferred_element_type=F32).astype(BF)
    decoded = scatter(
        term_a.reshape(NS, NX, NC, rows, half), term_b.reshape(NX, NS, NC, rows, half), core
    )
    def finish(total, own, bias):
        total = total + bias[None, :]
        return total.astype(BF), ((total - own.astype(F32)) * cot_scale).astype(BF)

    recon_b, cot_own_b = finish(decoded[1], tokens[:, half:], dec_bias[half:])
    own_a, _ = tie(tokens[:, :half], cot_own_b)
    recon_a, cot_own_a = finish(decoded[0], own_a, dec_bias[:half])
    cot_a, cot_b, slope = gather(cot_own_a, cot_own_b, core, slope)

    over_cols = (((1,), (1,)), ((), ()))
    over_rows = (((0,), (0,)), ((), ()))

    def product(left, right, dims):
        return lax.dot_general(left, right, dims, preferred_element_type=F32)

    dec_b = split_core(product(act_b, cot_b, over_rows).astype(BF), core)
    dec_a = split_core(product(act, cot_a, over_rows).astype(BF), core)
    dec_a, dec_b, cot_a, cot_b = tie(dec_a, dec_b, cot_a, cot_b)
    came_b, came_a = core_swap(dec_b[1]), core_swap(dec_a[1])
    grad = product(cot_a, dec_weight[:, :half], over_cols) + swapped(
        product(cot_b, dec_weight[:, half:], over_cols), NX, NS
    )
    came_a, came_b, grad = tie(came_a, came_b, grad)
    dec_chip = from_here(add(dec_a[0], came_a), add(dec_b[0], came_b))
    dec_up, dec_down = y_first(dec_chip)
    pre_grad = (grad * slope).astype(BF)
    pre_grad, pre_grad_b = tie(pre_grad, swapped(pre_grad, NS, NX))
    enc_b = split_core(product(pre_grad_b, tok_b, over_rows).astype(BF), core)
    enc_a = split_core(product(pre_grad, tok_a, over_rows).astype(BF), core)
    dec_up, dec_down, enc_a, enc_b = tie(dec_up, dec_down, enc_a, enc_b)
    dec_last = y_second(dec_chip, dec_up, dec_down)
    came_b, came_a = core_swap(enc_b[1]), core_swap(enc_a[1])
    enc_chip = from_here(add(enc_a[0], came_a), add(enc_b[0], came_b))
    enc_chip, dec_last = tie(enc_chip, dec_last)
    enc_up, enc_down = y_first(enc_chip)
    enc_last = y_second(enc_chip, enc_up, enc_down)
    dec_grad = y_total(dec_chip, dec_up, dec_down, *dec_last)
    enc_grad = y_total(enc_chip, enc_up, enc_down, *enc_last).T
    return (jnp.concatenate([recon_a, recon_b], axis=1), enc_grad, dec_grad)


def solution(mesh):
    placed = (
        P(("tok", "lat"), None),
        P(None, "lat"),
        P("lat"),
        P("lat", None),
        P(),
        P("tok", None),
    )
    return jax.shard_map(
        shards,
        mesh=mesh,
        in_specs=placed,
        out_specs=(P(("tok", "lat"), None), P("tok", "lat"), P("lat", "tok")),
        check_vma=False,
    )
```

```python
import math

import jax
import jax.numpy as jnp
from jax import lax
from jax.sharding import PartitionSpec as P

LB = 256
NX, NZ, NY, NC = 4, 8, 4, 2
NS = NZ // 2
BF = jnp.bfloat16
F32 = jnp.float32
BOTH = ("tok", "lat")


def index_of(y, c, x, z):
    return (((y % NY) * NC + c) * NX + x % NX) * NZ + z % NZ


def everywhere(cores=(0, 1)):
    return [
        (y, c, x, z) for y in range(NY) for c in cores for x in range(NX) for z in range(NZ)
    ]


def x_shift(value, step):
    pairs = [(index_of(y, c, x, z), index_of(y, c, x + step, z)) for y, c, x, z in everywhere()]
    return lax.ppermute(value, BOTH, pairs)


def y_shift(value, step):
    pairs = [(index_of(y, c, x, z), index_of(y + step, c, x, z)) for y, c, x, z in everywhere()]
    return lax.ppermute(value, BOTH, pairs)


def z_turn(value, step, cores=(0, 1)):
    pairs = [
        (index_of(y, c, x, z), index_of(y, c, x, z + (step if c == 0 else -step)))
        for y, c, x, z in everywhere(cores)
    ]
    return lax.ppermute(value, BOTH, pairs)


def core_swap(value):
    pairs = [(index_of(y, c, x, z), index_of(y, 1 - c, x, z)) for y, c, x, z in everywhere()]
    return lax.ppermute(value, BOTH, pairs)


def add(left, right):
    return (left.astype(F32) + right.astype(F32)).astype(BF)


def tie(*values):
    return lax.optimization_barrier(values)


def gather_head(own_a, own_b):
    chip_b = jnp.stack([own_b, core_swap(own_b)], axis=0)
    line = jnp.stack([own_a] + [x_shift(own_a, -k) for k in range(1, NX)], axis=0)
    return line, chip_b


def gather(line, chip_b, core, extra):
    first = core == 0
    width = line.shape[2]
    one, two = z_turn(chip_b, -1), z_turn(chip_b, -2)
    chip_a = jnp.stack([line, core_swap(line)], axis=1)
    step_1 = z_turn(chip_a, -1)
    near = jnp.stack([one, two], axis=0)
    far = z_turn(near, -2)
    near_1, near_3 = x_shift(near, -1), x_shift(near, 1)
    ends = jnp.stack([jnp.where(first, chip_b, far[1]), far[0]], axis=0)
    ends, step_1, near_1, near_3, extra = tie(ends, step_1, near_1, near_3, extra)
    ends_1, ends_3 = x_shift(ends, -1), x_shift(ends, 1)
    step_2 = z_turn(step_1, -1)
    ends_1, ends_3, step_2 = tie(ends_1, ends_3, step_2)
    near_2, ends_2 = x_shift(near_1, -1), x_shift(ends_3, 1)
    step_3 = z_turn(step_2, -1)
    step_4 = z_turn(step_3, -1, cores=(1,))
    whole_b = jnp.stack([ends, near, ends_1, near_1, ends_2, near_2, ends_3, near_3], axis=0)
    whole_a = jnp.stack([jnp.where(first, chip_a, step_4), step_3, step_1, step_2], axis=0)
    return whole_a.reshape(-1, width), whole_b.reshape(-1, width), extra


def scatter(terms_a, terms_b, core):
    first = core == 0
    ends = [terms_b[k, :2] for k in range(NX)]
    near = [terms_b[k, 2:] for k in range(NX)]
    ends_up, ends_far = x_shift(ends[1], 1), x_shift(ends[2], -1)
    step = z_turn(terms_a[0], 1, cores=(1,))
    ends_up, ends_far, step = tie(ends_up, ends_far, step)
    step, ends_far = tie(add(terms_a[1], step), ends_far)
    step = z_turn(step, 1)
    ends_down = x_shift(add(ends[3], ends_far), -1)
    near_far = x_shift(near[2], 1)
    ends_down, near_far, step = tie(ends_down, near_far, step)
    step, ends_down, near_far = tie(add(terms_a[3], step), ends_down, near_far)
    step = z_turn(step, 1)
    ends_sum = (ends[0].astype(F32) + ends_up.astype(F32) + ends_down.astype(F32)).astype(BF)
    far = z_turn(ends_sum, 2)
    near_up, near_down = x_shift(add(near[1], near_far), 1), x_shift(near[3], -1)
    far, near_up, near_down, step = tie(far, near_up, near_down, step)
    step, far, near_up, near_down = tie(add(terms_a[2], step), far, near_up, near_down)
    step = z_turn(step, 1)
    near_sum = near[0].astype(F32) + near_up.astype(F32) + near_down.astype(F32)
    one = z_turn(add(near_sum[0], far[1]), 1)
    two = z_turn(add(near_sum[1], jnp.where(first, jnp.zeros_like(far[0]), far[0])), 2)

    chip_a = step.astype(F32) + jnp.where(first, terms_a[0].astype(F32), 0.0)
    chip_b = one.astype(F32) + two.astype(F32) + jnp.where(first, ends_sum[0].astype(F32), 0.0)
    line = (chip_a[:, 0] + core_swap(chip_a[:, 1].astype(BF)).astype(F32)).astype(BF)
    came_b = core_swap(chip_b.astype(BF))
    total_b = chip_b + came_b[::-1].astype(F32)
    total_a = line.astype(F32)
    for k in range(1, NX):
        total_a = total_a + jnp.roll(x_shift(line, -k), k, axis=0).astype(F32)
    return total_a, total_b


def split_core(part, core):
    blocks = NY // 2
    block = part.shape[1] // (blocks * NC)

    def take(c):
        pieces = [
            lax.dynamic_slice_in_dim(part, (j * NC + c) * block, block, 1) for j in range(blocks)
        ]
        return jnp.stack(pieces, axis=0)

    return take(core), take(1 - core)


def from_here(low, high):
    whole = jnp.concatenate([low, high], axis=0)
    y_here = lax.axis_index("tok") // NC
    return jnp.stack(
        [lax.dynamic_index_in_dim(whole, (y_here + k) % NY, 0, keepdims=False) for k in range(NY)],
        axis=0,
    )


def y_first(chip):
    half = chip.shape[1] // 2
    return y_shift(chip[2, :half], 1), y_shift(chip[2, half:], -1)


def y_second(chip, far_up, far_down):
    half = chip.shape[1] // 2
    up = jnp.concatenate([add(chip[1, :half], far_up), chip[1, half:]], axis=0)
    down = jnp.concatenate([chip[3, :half], add(chip[3, half:], far_down)], axis=0)
    return y_shift(up, 1), y_shift(down, -1)


def y_total(chip, up, down):
    return chip[0].astype(F32) + up.astype(F32) + down.astype(F32)


def shards(tokens, enc_weight, enc_bias, dec_weight, dec_bias, active_blocks):
    rows, depth = tokens.shape
    latent_width = enc_weight.shape[1]
    half = depth // 2
    here = NS * NX * NC * rows
    cot_scale = 1.0 / math.sqrt(rows * NX * NZ * NY * NC)
    owner = lax.axis_index("lat")
    core = lax.axis_index("tok") % NC
    x_here = owner // NZ

    def swapped(rows_b, outer, inner):
        shaped = rows_b.reshape(outer, inner, NC * rows, -1)
        return jnp.swapaxes(shaped, 0, 1).reshape(here, -1)

    tok_line, tok_chip = gather_head(tokens[:, :half], tokens[:, half:])
    tok_a, tok_b, lists = gather(tok_line, tok_chip, core, active_blocks)

    lists = jnp.stack([lists, core_swap(lists)], axis=0)
    hits = jnp.any(lists == owner, axis=2).astype(F32)
    blocks = active_blocks.shape[0]
    x_block = ((x_here + jnp.arange(NX)) % NX) // (NX // blocks)
    gate = sum(jnp.where(x_block[:, None] == b, hits[None, :, b], 0.0) for b in range(blocks))
    gate = jnp.broadcast_to(gate[None, :, :, None], (NS, NX, NC, rows)).reshape(here, 1)

    pre_b = jnp.dot(tok_b, enc_weight[half:], preferred_element_type=F32)
    pre_act = jnp.dot(tok_a, enc_weight[:half], preferred_element_type=F32)
    pre_act = pre_act + swapped(pre_b, NX, NS) + enc_bias[None, :]
    act = (jax.nn.silu(pre_act) * gate).astype(BF)
    act_b = swapped(act, NS, NX)
    sigma = jax.nn.sigmoid(pre_act)
    slope = sigma * (1.0 + pre_act * (1.0 - sigma)) * gate
    act, act_b, slope = tie(act, act_b, slope)

    term_b = jnp.dot(act_b, dec_weight[:, half:], preferred_element_type=F32).astype(BF)
    term_a = jnp.dot(act, dec_weight[:, :half], preferred_element_type=F32).astype(BF)
    decoded = scatter(
        term_a.reshape(NS, NX, NC, rows, half), term_b.reshape(NX, NS, NC, rows, half), core
    )
    def finish(total, own, bias):
        total = total + bias[None, None, :]
        return total[0].astype(BF), ((total - own.astype(F32)) * cot_scale).astype(BF)

    recon_b, cot_chip = finish(decoded[1], tok_chip, dec_bias[half:])
    recon_a, cot_line = finish(decoded[0], tok_line, dec_bias[:half])
    cot_a, cot_b, slope = gather(cot_line, cot_chip, core, slope)

    over_cols = (((1,), (1,)), ((), ()))
    over_rows = (((0,), (0,)), ((), ()))

    def product(left, right, dims):
        return lax.dot_general(left, right, dims, preferred_element_type=F32)

    dec_b = split_core(product(act_b, cot_b, over_rows).astype(BF), core)
    dec_a = split_core(product(act, cot_a, over_rows).astype(BF), core)
    dec_a, dec_b, cot_a, cot_b = tie(dec_a, dec_b, cot_a, cot_b)
    came_b, came_a = core_swap(dec_b[1]), core_swap(dec_a[1])
    grad = product(cot_a, dec_weight[:, :half], over_cols) + swapped(
        product(cot_b, dec_weight[:, half:], over_cols), NX, NS
    )
    came_a, came_b, grad = tie(came_a, came_b, grad)
    dec_chip = from_here(add(dec_a[0], came_a), add(dec_b[0], came_b))
    dec_far = y_first(dec_chip)
    pre_grad = (grad * slope).astype(BF)
    pre_grad, pre_grad_b = tie(pre_grad, swapped(pre_grad, NS, NX))
    enc_b = split_core(product(pre_grad_b, tok_b, over_rows).astype(BF), core)
    enc_a = split_core(product(pre_grad, tok_a, over_rows).astype(BF), core)
    dec_far, enc_a, enc_b = tie(dec_far, enc_a, enc_b)
    dec_both = y_second(dec_chip, *dec_far)
    came_b, came_a = core_swap(enc_b[1]), core_swap(enc_a[1])
    enc_chip = from_here(add(enc_a[0], came_a), add(enc_b[0], came_b))
    enc_far = y_first(enc_chip)
    enc_far, dec_both = tie(enc_far, dec_both)
    enc_both = y_second(enc_chip, *enc_far)
    dec_grad = y_total(dec_chip, *dec_both)
    enc_grad = y_total(enc_chip, *enc_both).T
    return (jnp.concatenate([recon_a, recon_b], axis=1), enc_grad, dec_grad)


def solution(mesh):
    placed = (
        P(("tok", "lat"), None),
        P(None, "lat"),
        P("lat"),
        P("lat", None),
        P(),
        P("tok", None),
    )
    return jax.shard_map(
        shards,
        mesh=mesh,
        in_specs=placed,
        out_specs=(P(("tok", "lat"), None), P("tok", "lat"), P("lat", "tok")),
        check_vma=False,
    )
```

```python
import math

import jax
import jax.numpy as jnp
from jax import lax
from jax.sharding import PartitionSpec as P

LB = 256
NX, NZ, NY, NC = 4, 8, 4, 2
NS = NZ // 2
BF = jnp.bfloat16
F32 = jnp.float32
BOTH = ("tok", "lat")


def index_of(y, c, x, z):
    return (((y % NY) * NC + c) * NX + x % NX) * NZ + z % NZ


def everywhere(cores=(0, 1)):
    return [
        (y, c, x, z) for y in range(NY) for c in cores for x in range(NX) for z in range(NZ)
    ]


def x_shift(value, step):
    pairs = [(index_of(y, c, x, z), index_of(y, c, x + step, z)) for y, c, x, z in everywhere()]
    return lax.ppermute(value, BOTH, pairs)


def y_shift(value, step):
    pairs = [(index_of(y, c, x, z), index_of(y + step, c, x, z)) for y, c, x, z in everywhere()]
    return lax.ppermute(value, BOTH, pairs)


def z_turn(value, step, cores=(0, 1)):
    pairs = [
        (index_of(y, c, x, z), index_of(y, c, x, z + (step if c == 0 else -step)))
        for y, c, x, z in everywhere(cores)
    ]
    return lax.ppermute(value, BOTH, pairs)


def core_swap(value):
    pairs = [(index_of(y, c, x, z), index_of(y, 1 - c, x, z)) for y, c, x, z in everywhere()]
    return lax.ppermute(value, BOTH, pairs)


def add(left, right):
    return (left.astype(F32) + right.astype(F32)).astype(BF)


def tie(*values):
    return lax.optimization_barrier(values)


def gather_head(own_a, own_b):
    chip_b = jnp.stack([own_b, core_swap(own_b)], axis=0)
    line = jnp.stack([own_a] + [x_shift(own_a, -k) for k in range(1, NX)], axis=0)
    return line, chip_b


def gather(line, chip_b, core, extra):
    first = core == 0
    width = line.shape[2]
    one, two = z_turn(chip_b, -1), z_turn(chip_b, -2)
    chip_a = jnp.stack([line, core_swap(line)], axis=1)
    step_1 = z_turn(chip_a, -1)
    near = jnp.stack([one, two], axis=0)
    far = z_turn(near, -2)
    near_1, near_3 = x_shift(near, -1), x_shift(near, 1)
    ends = jnp.stack([jnp.where(first, chip_b, far[1]), far[0]], axis=0)
    ends, step_1, near_1, near_3, extra = tie(ends, step_1, near_1, near_3, extra)
    step_2 = z_turn(step_1, -1)
    ends_1, ends_3 = x_shift(ends, -1), x_shift(ends, 1)
    near_2 = x_shift(near_1, -1)
    step_2, ends_1, ends_3 = tie(step_2, ends_1, ends_3)
    step_3 = z_turn(step_2, -1)
    ends_2 = x_shift(ends_3, 1)
    step_4 = z_turn(step_3, -1, cores=(1,))
    whole_a = jnp.stack([jnp.where(first, chip_a, step_4), step_3, step_1, step_2], axis=0)
    ends_b = jnp.stack([ends, ends_1, ends_2, ends_3], axis=0)
    near_b = jnp.stack([near, near_1, near_2, near_3], axis=0)
    return whole_a.reshape(-1, width), (ends_b.reshape(-1, width), near_b.reshape(-1, width)), extra


def scatter(terms_a, ends, near, core):
    first = core == 0
    ends_up, ends_far = x_shift(ends[1], 1), x_shift(ends[2], -1)
    step = z_turn(terms_a[0], 1, cores=(1,))
    ends_up, ends_far, step = tie(ends_up, ends_far, step)
    step, ends_far = tie(add(terms_a[1], step), ends_far)
    step = z_turn(step, 1)
    ends_down = x_shift(add(ends[3], ends_far), -1)
    near_far = x_shift(near[2], 1)
    ends_down, near_far, step = tie(ends_down, near_far, step)
    step, ends_down, near_far = tie(add(terms_a[3], step), ends_down, near_far)
    step = z_turn(step, 1)
    ends_sum = (ends[0].astype(F32) + ends_up.astype(F32) + ends_down.astype(F32)).astype(BF)
    far = z_turn(ends_sum, 2)
    near_up, near_down = x_shift(add(near[1], near_far), 1), x_shift(near[3], -1)
    far, near_up, near_down, step = tie(far, near_up, near_down, step)
    step, far, near_up, near_down = tie(add(terms_a[2], step), far, near_up, near_down)
    step = z_turn(step, 1)
    near_sum = near[0].astype(F32) + near_up.astype(F32) + near_down.astype(F32)
    one = z_turn(add(near_sum[0], far[1]), 1)
    two = z_turn(add(near_sum[1], jnp.where(first, jnp.zeros_like(far[0]), far[0])), 2)

    chip_a = step.astype(F32) + jnp.where(first, terms_a[0].astype(F32), 0.0)
    chip_b = one.astype(F32) + two.astype(F32) + jnp.where(first, ends_sum[0].astype(F32), 0.0)
    line = (chip_a[:, 0] + core_swap(chip_a[:, 1].astype(BF)).astype(F32)).astype(BF)
    came_b = core_swap(chip_b.astype(BF))
    total_b = chip_b + came_b[::-1].astype(F32)
    total_a = line.astype(F32)
    for k in range(1, NX):
        total_a = total_a + jnp.roll(x_shift(line, -k), k, axis=0).astype(F32)
    return total_a, total_b


def split_core(part, core):
    blocks = NY // 2
    block = part.shape[1] // (blocks * NC)

    def take(c):
        pieces = [
            lax.dynamic_slice_in_dim(part, (j * NC + c) * block, block, 1) for j in range(blocks)
        ]
        return jnp.stack(pieces, axis=0)

    return take(core), take(1 - core)


def from_here(low, high):
    whole = jnp.concatenate([low, high], axis=0)
    y_here = lax.axis_index("tok") // NC
    return jnp.stack(
        [lax.dynamic_index_in_dim(whole, (y_here + k) % NY, 0, keepdims=False) for k in range(NY)],
        axis=0,
    )


def y_first(chip):
    half = chip.shape[1] // 2
    return y_shift(chip[2, :half], 1), y_shift(chip[2, half:], -1)


def y_second(chip, far_up, far_down):
    half = chip.shape[1] // 2
    up = jnp.concatenate([add(chip[1, :half], far_up), chip[1, half:]], axis=0)
    down = jnp.concatenate([chip[3, :half], add(chip[3, half:], far_down)], axis=0)
    return y_shift(up, 1), y_shift(down, -1)


def y_total(chip, up, down):
    return chip[0].astype(F32) + up.astype(F32) + down.astype(F32)


def shards(tokens, enc_weight, enc_bias, dec_weight, dec_bias, active_blocks):
    rows, depth = tokens.shape
    latent_width = enc_weight.shape[1]
    half = depth // 2
    here = NS * NX * NC * rows
    cot_scale = 1.0 / math.sqrt(rows * NX * NZ * NY * NC)
    owner = lax.axis_index("lat")
    core = lax.axis_index("tok") % NC
    x_here = owner // NZ

    def swapped(part, outer, inner):
        shaped = part.reshape(outer, inner, NC * rows, -1)
        return jnp.swapaxes(shaped, 0, 1).reshape(part.shape)

    def as_a(ends, near):
        return jnp.concatenate([swapped(ends, NX, 2), swapped(near, NX, 2)], axis=0)

    def as_b(whole):
        return swapped(whole[: here // 2], 2, NX), swapped(whole[here // 2 :], 2, NX)

    tok_line, tok_chip = gather_head(tokens[:, :half], tokens[:, half:])
    tok_a, tok_b, lists = gather(tok_line, tok_chip, core, active_blocks)

    lists = jnp.stack([lists, core_swap(lists)], axis=0)
    hits = jnp.any(lists == owner, axis=2).astype(F32)
    blocks = active_blocks.shape[0]
    x_block = ((x_here + jnp.arange(NX)) % NX) // (NX // blocks)
    gate = sum(jnp.where(x_block[:, None] == b, hits[None, :, b], 0.0) for b in range(blocks))
    gate = jnp.broadcast_to(gate[None, :, :, None], (NS, NX, NC, rows)).reshape(here, 1)

    enc_low, enc_high = enc_weight[:half], enc_weight[half:]
    dec_low, dec_high = dec_weight[:, :half], dec_weight[:, half:]
    pre_b = [jnp.dot(part, enc_high, preferred_element_type=F32) for part in tok_b]
    pre_act = jnp.dot(tok_a, enc_low, preferred_element_type=F32)
    pre_act = pre_act + as_a(*pre_b) + enc_bias[None, :]
    act = (jax.nn.silu(pre_act) * gate).astype(BF)
    act_b = as_b(act)
    sigma = jax.nn.sigmoid(pre_act)
    slope = sigma * (1.0 + pre_act * (1.0 - sigma)) * gate
    act, act_b, slope = tie(act, act_b, slope)

    ends, near = [
        jnp.dot(part, dec_high, preferred_element_type=F32)
        .astype(BF)
        .reshape(NX, 2, NC, rows, half)
        for part in act_b
    ]
    term_a = jnp.dot(act, dec_low, preferred_element_type=F32).astype(BF)
    decoded = scatter(term_a.reshape(NS, NX, NC, rows, half), ends, near, core)

    def finish(total, own, bias):
        total = total + bias[None, None, :]
        return total[0].astype(BF), ((total - own.astype(F32)) * cot_scale).astype(BF)

    recon_b, cot_chip = finish(decoded[1], tok_chip, dec_bias[half:])
    recon_a, cot_line = finish(decoded[0], tok_line, dec_bias[:half])
    cot_a, cot_b, slope = gather(cot_line, cot_chip, core, slope)

    over_cols = (((1,), (1,)), ((), ()))
    over_rows = (((0,), (0,)), ((), ()))

    def product(left, right, dims):
        return lax.dot_general(left, right, dims, preferred_element_type=F32)

    def pair_sum(left, right):
        return product(left[0], right[0], over_rows) + product(left[1], right[1], over_rows)

    dec_b = split_core(pair_sum(act_b, cot_b).astype(BF), core)
    dec_a = split_core(product(act, cot_a, over_rows).astype(BF), core)
    dec_a, dec_b, cot_a, cot_b = tie(dec_a, dec_b, cot_a, cot_b)
    came_b, came_a = core_swap(dec_b[1]), core_swap(dec_a[1])
    grad = product(cot_a, dec_low, over_cols) + as_a(
        *[product(part, dec_high, over_cols) for part in cot_b]
    )
    came_a, came_b, grad = tie(came_a, came_b, grad)
    dec_chip = from_here(add(dec_a[0], came_a), add(dec_b[0], came_b))
    dec_far = y_first(dec_chip)
    pre_grad = (grad * slope).astype(BF)
    pre_grad, pre_grad_b = tie(pre_grad, as_b(pre_grad))
    enc_b = split_core(pair_sum(pre_grad_b, tok_b).astype(BF), core)
    enc_a = split_core(product(pre_grad, tok_a, over_rows).astype(BF), core)
    dec_far, enc_a, enc_b = tie(dec_far, enc_a, enc_b)
    dec_both = y_second(dec_chip, *dec_far)
    came_b, came_a = core_swap(enc_b[1]), core_swap(enc_a[1])
    enc_chip = from_here(add(enc_a[0], came_a), add(enc_b[0], came_b))
    enc_far = y_first(enc_chip)
    enc_far, dec_both = tie(enc_far, dec_both)
    enc_both = y_second(enc_chip, *enc_far)
    dec_grad = y_total(dec_chip, *dec_both)
    enc_grad = y_total(enc_chip, *enc_both).T
    return (jnp.concatenate([recon_a, recon_b], axis=1), enc_grad, dec_grad)


def solution(mesh):
    placed = (
        P(("tok", "lat"), None),
        P(None, "lat"),
        P("lat"),
        P("lat", None),
        P(),
        P("tok", None),
    )
    return jax.shard_map(
        shards,
        mesh=mesh,
        in_specs=placed,
        out_specs=(P(("tok", "lat"), None), P("tok", "lat"), P("lat", "tok")),
        check_vma=False,
    )
```

```python
import math

import jax
import jax.numpy as jnp
from jax import lax
from jax.sharding import PartitionSpec as P

LB = 256
NX, NZ, NY, NC = 4, 8, 4, 2
NS = NZ // 2
BF = jnp.bfloat16
F32 = jnp.float32
BOTH = ("tok", "lat")


def index_of(y, c, x, z):
    return (((y % NY) * NC + c) * NX + x % NX) * NZ + z % NZ


def everywhere(cores=(0, 1)):
    return [
        (y, c, x, z) for y in range(NY) for c in cores for x in range(NX) for z in range(NZ)
    ]


def x_shift(value, step):
    pairs = [(index_of(y, c, x, z), index_of(y, c, x + step, z)) for y, c, x, z in everywhere()]
    return lax.ppermute(value, BOTH, pairs)


def y_shift(value, step):
    pairs = [(index_of(y, c, x, z), index_of(y + step, c, x, z)) for y, c, x, z in everywhere()]
    return lax.ppermute(value, BOTH, pairs)


def z_turn(value, step, cores=(0, 1)):
    pairs = [
        (index_of(y, c, x, z), index_of(y, c, x, z + (step if c == 0 else -step)))
        for y, c, x, z in everywhere(cores)
    ]
    return lax.ppermute(value, BOTH, pairs)


def core_swap(value):
    pairs = [(index_of(y, c, x, z), index_of(y, 1 - c, x, z)) for y, c, x, z in everywhere()]
    return lax.ppermute(value, BOTH, pairs)


def add(left, right):
    return (left.astype(F32) + right.astype(F32)).astype(BF)


def tie(*values):
    return lax.optimization_barrier(values)


def gather_head(own_a, own_b):
    chip_b = jnp.stack([own_b, core_swap(own_b)], axis=0)
    line = jnp.stack([own_a] + [x_shift(own_a, -k) for k in range(1, NX)], axis=0)
    return line, chip_b


def gather(line, chip_b, core, extra):
    first = core == 0
    width = line.shape[2]
    one, two = z_turn(chip_b, -1), z_turn(chip_b, -2)
    chip_a = jnp.stack([line, core_swap(line)], axis=1)
    step_1 = z_turn(chip_a, -1)
    near = jnp.stack([one, two], axis=0)
    far = z_turn(near, -2)
    near_1, near_3 = x_shift(near, -1), x_shift(near, 1)
    ends = jnp.stack([jnp.where(first, chip_b, far[1]), far[0]], axis=0)
    ends, step_1, near_1, near_3, extra = tie(ends, step_1, near_1, near_3, extra)
    step_2 = z_turn(step_1, -1)
    ends_1, ends_3 = x_shift(ends, -1), x_shift(ends, 1)
    step_2, ends_1, ends_3, near_1 = tie(step_2, ends_1, ends_3, near_1)
    step_3 = z_turn(step_2, -1)
    ends_2, near_2 = x_shift(ends_3, 1), x_shift(near_1, -1)
    step_3, ends_2, near_2 = tie(step_3, ends_2, near_2)
    step_4 = z_turn(step_3, -1, cores=(1,))
    whole_a = jnp.stack([jnp.where(first, chip_a, step_4), step_3, step_1, step_2], axis=0)
    ends_b = jnp.stack([ends, ends_1, ends_2, ends_3], axis=0)
    near_b = jnp.stack([near, near_1, near_2, near_3], axis=0)
    return whole_a.reshape(-1, width), (ends_b.reshape(-1, width), near_b.reshape(-1, width)), extra


def scatter(terms_a, ends, near, core):
    first = core == 0
    ends_up, ends_far = x_shift(ends[1], 1), x_shift(ends[2], -1)
    step = z_turn(terms_a[0], 1, cores=(1,))
    ends_up, ends_far, step = tie(ends_up, ends_far, step)
    step, ends_far = tie(add(terms_a[1], step), ends_far)
    step = z_turn(step, 1)
    ends_down = x_shift(add(ends[3], ends_far), -1)
    near_far = x_shift(near[2], 1)
    ends_down, near_far, step = tie(ends_down, near_far, step)
    step, ends_down, near_far = tie(add(terms_a[3], step), ends_down, near_far)
    step = z_turn(step, 1)
    ends_sum = (ends[0].astype(F32) + ends_up.astype(F32) + ends_down.astype(F32)).astype(BF)
    far = z_turn(ends_sum, 2)
    near_up, near_down = x_shift(add(near[1], near_far), 1), x_shift(near[3], -1)
    far, near_up, near_down, step = tie(far, near_up, near_down, step)
    step, far, near_up, near_down = tie(add(terms_a[2], step), far, near_up, near_down)
    step = z_turn(step, 1)
    near_sum = near[0].astype(F32) + near_up.astype(F32) + near_down.astype(F32)
    one = z_turn(add(near_sum[0], far[1]), 1)
    two = z_turn(add(near_sum[1], jnp.where(first, jnp.zeros_like(far[0]), far[0])), 2)

    chip_a = step.astype(F32) + jnp.where(first, terms_a[0].astype(F32), 0.0)
    chip_b = one.astype(F32) + two.astype(F32) + jnp.where(first, ends_sum[0].astype(F32), 0.0)
    line = (chip_a[:, 0] + core_swap(chip_a[:, 1].astype(BF)).astype(F32)).astype(BF)
    came_b = core_swap(chip_b.astype(BF))
    total_b = chip_b + came_b[::-1].astype(F32)
    total_a = line.astype(F32)
    for k in range(1, NX):
        total_a = total_a + jnp.roll(x_shift(line, -k), k, axis=0).astype(F32)
    return total_a, total_b


def split_core(part, core):
    blocks = NY // 2
    block = part.shape[1] // (blocks * NC)

    def take(c):
        pieces = [
            lax.dynamic_slice_in_dim(part, (j * NC + c) * block, block, 1) for j in range(blocks)
        ]
        return jnp.stack(pieces, axis=0)

    return take(core), take(1 - core)


def from_here(low, high):
    whole = jnp.concatenate([low, high], axis=0)
    y_here = lax.axis_index("tok") // NC
    return jnp.stack(
        [lax.dynamic_index_in_dim(whole, (y_here + k) % NY, 0, keepdims=False) for k in range(NY)],
        axis=0,
    )


def y_first(chip):
    half = chip.shape[1] // 2
    return y_shift(chip[2, :half], 1), y_shift(chip[2, half:], -1)


def y_second(chip, far_up, far_down):
    half = chip.shape[1] // 2
    up = jnp.concatenate([add(chip[1, :half], far_up), chip[1, half:]], axis=0)
    down = jnp.concatenate([chip[3, :half], add(chip[3, half:], far_down)], axis=0)
    return y_shift(up, 1), y_shift(down, -1)


def y_total(chip, up, down):
    return chip[0].astype(F32) + up.astype(F32) + down.astype(F32)


def shards(tokens, enc_weight, enc_bias, dec_weight, dec_bias, active_blocks):
    rows, depth = tokens.shape
    latent_width = enc_weight.shape[1]
    half = depth // 2
    here = NS * NX * NC * rows
    cot_scale = 1.0 / math.sqrt(rows * NX * NZ * NY * NC)
    owner = lax.axis_index("lat")
    core = lax.axis_index("tok") % NC
    x_here = owner // NZ

    def swapped(part, outer, inner):
        shaped = part.reshape(outer, inner, NC * rows, -1)
        return jnp.swapaxes(shaped, 0, 1).reshape(part.shape)

    def as_a(ends, near):
        return jnp.concatenate([swapped(ends, NX, 2), swapped(near, NX, 2)], axis=0)

    def as_b(whole):
        return swapped(whole[: here // 2], 2, NX), swapped(whole[here // 2 :], 2, NX)

    lists = jnp.stack([active_blocks, core_swap(active_blocks)], axis=0)
    hits = jnp.any(lists == owner, axis=2).astype(F32)
    blocks = active_blocks.shape[0]
    x_block = ((x_here + jnp.arange(NX)) % NX) // (NX // blocks)
    gate = sum(jnp.where(x_block[:, None] == b, hits[None, :, b], 0.0) for b in range(blocks))
    gate = jnp.broadcast_to(gate[None, :, :, None], (NS, NX, NC, rows)).reshape(here, 1)

    tok_line, tok_chip = gather_head(tokens[:, :half], tokens[:, half:])
    tok_a, tok_b, gate = gather(tok_line, tok_chip, core, gate)

    enc_low, enc_high = enc_weight[:half], enc_weight[half:]
    dec_low, dec_high = dec_weight[:, :half], dec_weight[:, half:]
    pre_b = [jnp.dot(part, enc_high, preferred_element_type=F32) for part in tok_b]
    pre_act = jnp.dot(tok_a, enc_low, preferred_element_type=F32)
    pre_act = pre_act + as_a(*pre_b) + enc_bias[None, :]
    act = (jax.nn.silu(pre_act) * gate).astype(BF)
    act_b = as_b(act)
    sigma = jax.nn.sigmoid(pre_act)
    slope = sigma * (1.0 + pre_act * (1.0 - sigma)) * gate
    act, act_b, slope = tie(act, act_b, slope)

    ends, near = [
        jnp.dot(part, dec_high, preferred_element_type=F32)
        .astype(BF)
        .reshape(NX, 2, NC, rows, half)
        for part in act_b
    ]
    term_a = jnp.dot(act, dec_low, preferred_element_type=F32).astype(BF)
    decoded = scatter(term_a.reshape(NS, NX, NC, rows, half), ends, near, core)

    def finish(total, own, bias):
        total = total + bias[None, None, :]
        return total[0].astype(BF), ((total - own.astype(F32)) * cot_scale).astype(BF)

    recon_b, cot_chip = finish(decoded[1], tok_chip, dec_bias[half:])
    recon_a, cot_line = finish(decoded[0], tok_line, dec_bias[:half])
    cot_a, cot_b, slope = gather(cot_line, cot_chip, core, slope)

    over_cols = (((1,), (1,)), ((), ()))
    over_rows = (((0,), (0,)), ((), ()))

    def product(left, right, dims):
        return lax.dot_general(left, right, dims, preferred_element_type=F32)

    def pair_sum(left, right):
        return product(left[0], right[0], over_rows) + product(left[1], right[1], over_rows)

    dec_b = split_core(pair_sum(act_b, cot_b).astype(BF), core)
    dec_a = split_core(product(act, cot_a, over_rows).astype(BF), core)
    dec_a, cot_a, cot_b = tie(dec_a, cot_a, cot_b)
    came_b, came_a = core_swap(dec_b[1]), core_swap(dec_a[1])
    grad = product(cot_a, dec_low, over_cols) + as_a(
        *[product(part, dec_high, over_cols) for part in cot_b]
    )
    came_a, came_b, grad = tie(came_a, came_b, grad)
    dec_chip = from_here(add(dec_a[0], came_a), add(dec_b[0], came_b))
    dec_far = y_first(dec_chip)
    pre_grad = (grad * slope).astype(BF)
    pre_grad, pre_grad_b = tie(pre_grad, as_b(pre_grad))
    enc_b = split_core(pair_sum(pre_grad_b, tok_b).astype(BF), core)
    enc_a = split_core(product(pre_grad, tok_a, over_rows).astype(BF), core)
    dec_far, enc_a, enc_b = tie(dec_far, enc_a, enc_b)
    dec_both = y_second(dec_chip, *dec_far)
    came_b, came_a = core_swap(enc_b[1]), core_swap(enc_a[1])
    enc_chip = from_here(add(enc_a[0], came_a), add(enc_b[0], came_b))
    enc_far = y_first(enc_chip)
    enc_far, dec_both = tie(enc_far, dec_both)
    enc_both = y_second(enc_chip, *enc_far)
    dec_grad = y_total(dec_chip, *dec_both)
    enc_grad = y_total(enc_chip, *enc_both).T
    return (jnp.concatenate([recon_a, recon_b], axis=1), enc_grad, dec_grad)


def solution(mesh):
    placed = (
        P(("tok", "lat"), None),
        P(None, "lat"),
        P("lat"),
        P("lat", None),
        P(),
        P("tok", None),
    )
    return jax.shard_map(
        shards,
        mesh=mesh,
        in_specs=placed,
        out_specs=(P(("tok", "lat"), None), P("tok", "lat"), P("lat", "tok")),
        check_vma=False,
    )
```

```python
import math

import jax
import jax.numpy as jnp
from jax import lax
from jax.sharding import PartitionSpec as P

LB = 256
NX, NZ, NY, NC = 4, 8, 4, 2
NS = NZ // 2
BF = jnp.bfloat16
F32 = jnp.float32
BOTH = ("tok", "lat")


def index_of(y, c, x, z):
    return (((y % NY) * NC + c) * NX + x % NX) * NZ + z % NZ


def everywhere(cores=(0, 1)):
    return [
        (y, c, x, z) for y in range(NY) for c in cores for x in range(NX) for z in range(NZ)
    ]


def x_shift(value, step):
    pairs = [(index_of(y, c, x, z), index_of(y, c, x + step, z)) for y, c, x, z in everywhere()]
    return lax.ppermute(value, BOTH, pairs)


def y_shift(value, step):
    pairs = [(index_of(y, c, x, z), index_of(y + step, c, x, z)) for y, c, x, z in everywhere()]
    return lax.ppermute(value, BOTH, pairs)


def z_turn(value, step, cores=(0, 1)):
    pairs = [
        (index_of(y, c, x, z), index_of(y, c, x, z + (step if c == 0 else -step)))
        for y, c, x, z in everywhere(cores)
    ]
    return lax.ppermute(value, BOTH, pairs)


def core_swap(value):
    pairs = [(index_of(y, c, x, z), index_of(y, 1 - c, x, z)) for y, c, x, z in everywhere()]
    return lax.ppermute(value, BOTH, pairs)


def add(left, right):
    return (left.astype(F32) + right.astype(F32)).astype(BF)


def tie(*values):
    return lax.optimization_barrier(values)


def gather_head(own_a, own_b):
    chip_b = jnp.stack([own_b, core_swap(own_b)], axis=0)
    line = jnp.stack([own_a] + [x_shift(own_a, -k) for k in range(1, NX)], axis=0)
    return line, chip_b


def gather(line, chip_b, core, extra):
    first = core == 0
    width = line.shape[2]
    one, two = z_turn(chip_b, -1), z_turn(chip_b, -2)
    chip_a = jnp.stack([line, core_swap(line)], axis=1)
    near = jnp.stack([one, two], axis=0)
    far = z_turn(near, -2)
    chip_a, near = tie(chip_a, near)
    step_1 = z_turn(chip_a, -1)
    near_1, near_3 = x_shift(near, -1), x_shift(near, 1)
    ends = jnp.stack([jnp.where(first, chip_b, far[1]), far[0]], axis=0)
    ends, step_1, near_1, near_3, extra = tie(ends, step_1, near_1, near_3, extra)
    step_2 = z_turn(step_1, -1)
    ends_1, ends_3 = x_shift(ends, -1), x_shift(ends, 1)
    near_2 = x_shift(near_1, -1)
    step_2, ends_1, ends_3 = tie(step_2, ends_1, ends_3)
    step_3 = z_turn(step_2, -1)
    ends_2 = x_shift(ends_3, 1)
    step_4 = z_turn(step_3, -1, cores=(1,))
    whole_a = jnp.stack([jnp.where(first, chip_a, step_4), step_3, step_1, step_2], axis=0)
    ends_b = jnp.stack([ends, ends_1, ends_2, ends_3], axis=0)
    near_b = jnp.stack([near, near_1, near_2, near_3], axis=0)
    return whole_a.reshape(-1, width), (ends_b.reshape(-1, width), near_b.reshape(-1, width)), extra


def scatter(terms_a, ends, near, core):
    first = core == 0
    ends_up, ends_far = x_shift(ends[1], 1), x_shift(ends[2], -1)
    step = z_turn(terms_a[0], 1, cores=(1,))
    ends_up, ends_far, step = tie(ends_up, ends_far, step)
    step, ends_far = tie(add(terms_a[1], step), ends_far)
    step = z_turn(step, 1)
    ends_down = x_shift(add(ends[3], ends_far), -1)
    near_far = x_shift(near[2], 1)
    ends_down, near_far, step = tie(ends_down, near_far, step)
    step, ends_down, near_far = tie(add(terms_a[3], step), ends_down, near_far)
    step = z_turn(step, 1)
    ends_sum = (ends[0].astype(F32) + ends_up.astype(F32) + ends_down.astype(F32)).astype(BF)
    far = z_turn(ends_sum, 2)
    near_up, near_down = x_shift(add(near[1], near_far), 1), x_shift(near[3], -1)
    far, near_up, near_down, step = tie(far, near_up, near_down, step)
    step, far, near_up, near_down = tie(add(terms_a[2], step), far, near_up, near_down)
    step = z_turn(step, 1)
    near_sum = near[0].astype(F32) + near_up.astype(F32) + near_down.astype(F32)
    one = z_turn(add(near_sum[0], far[1]), 1)
    two = z_turn(add(near_sum[1], jnp.where(first, jnp.zeros_like(far[0]), far[0])), 2)

    chip_a = step.astype(F32) + jnp.where(first, terms_a[0].astype(F32), 0.0)
    chip_b = one.astype(F32) + two.astype(F32) + jnp.where(first, ends_sum[0].astype(F32), 0.0)
    line = (chip_a[:, 0] + core_swap(chip_a[:, 1].astype(BF)).astype(F32)).astype(BF)
    came_b = core_swap(chip_b.astype(BF))
    total_b = chip_b + came_b[::-1].astype(F32)
    total_a = line.astype(F32)
    for k in range(1, NX):
        total_a = total_a + jnp.roll(x_shift(line, -k), k, axis=0).astype(F32)
    return total_a, total_b


def split_core(part, core):
    blocks = NY // 2
    block = part.shape[1] // (blocks * NC)

    def take(c):
        pieces = [
            lax.dynamic_slice_in_dim(part, (j * NC + c) * block, block, 1) for j in range(blocks)
        ]
        return jnp.stack(pieces, axis=0)

    return take(core), take(1 - core)


def from_here(low, high):
    whole = jnp.concatenate([low, high], axis=0)
    y_here = lax.axis_index("tok") // NC
    return jnp.stack(
        [lax.dynamic_index_in_dim(whole, (y_here + k) % NY, 0, keepdims=False) for k in range(NY)],
        axis=0,
    )


def y_first(chip):
    half = chip.shape[1] // 2
    return y_shift(chip[2, :half], 1), y_shift(chip[2, half:], -1)


def y_second(chip, far_up, far_down):
    half = chip.shape[1] // 2
    up = jnp.concatenate([add(chip[1, :half], far_up), chip[1, half:]], axis=0)
    down = jnp.concatenate([chip[3, :half], add(chip[3, half:], far_down)], axis=0)
    return y_shift(up, 1), y_shift(down, -1)


def y_total(chip, up, down):
    return chip[0].astype(F32) + up.astype(F32) + down.astype(F32)


def shards(tokens, enc_weight, enc_bias, dec_weight, dec_bias, active_blocks):
    rows, depth = tokens.shape
    latent_width = enc_weight.shape[1]
    half = depth // 2
    here = NS * NX * NC * rows
    cot_scale = 1.0 / math.sqrt(rows * NX * NZ * NY * NC)
    owner = lax.axis_index("lat")
    core = lax.axis_index("tok") % NC
    x_here = owner // NZ

    def swapped(part, outer, inner):
        shaped = part.reshape(outer, inner, NC * rows, -1)
        return jnp.swapaxes(shaped, 0, 1).reshape(part.shape)

    def as_a(ends, near):
        return jnp.concatenate([swapped(ends, NX, 2), swapped(near, NX, 2)], axis=0)

    def as_b(whole):
        return swapped(whole[: here // 2], 2, NX), swapped(whole[here // 2 :], 2, NX)

    tok_line, tok_chip = gather_head(tokens[:, :half], tokens[:, half:])
    tok_a, tok_b, lists = gather(tok_line, tok_chip, core, active_blocks)

    lists = jnp.stack([lists, core_swap(lists)], axis=0)
    hits = jnp.any(lists == owner, axis=2).astype(F32)
    blocks = active_blocks.shape[0]
    x_block = ((x_here + jnp.arange(NX)) % NX) // (NX // blocks)
    gate = sum(jnp.where(x_block[:, None] == b, hits[None, :, b], 0.0) for b in range(blocks))
    gate = jnp.broadcast_to(gate[None, :, :, None], (NS, NX, NC, rows)).reshape(here, 1)

    enc_low, enc_high = enc_weight[:half], enc_weight[half:]
    dec_low, dec_high = dec_weight[:, :half], dec_weight[:, half:]
    pre_b = [jnp.dot(part, enc_high, preferred_element_type=F32) for part in tok_b]
    pre_act = jnp.dot(tok_a, enc_low, preferred_element_type=F32)
    pre_act = pre_act + as_a(*pre_b) + enc_bias[None, :]
    act = (jax.nn.silu(pre_act) * gate).astype(BF)
    act_b = as_b(act)
    sigma = jax.nn.sigmoid(pre_act)
    slope = sigma * (1.0 + pre_act * (1.0 - sigma)) * gate
    act, act_b, slope = tie(act, act_b, slope)

    ends, near = [
        jnp.dot(part, dec_high, preferred_element_type=F32)
        .astype(BF)
        .reshape(NX, 2, NC, rows, half)
        for part in act_b
    ]
    term_a = jnp.dot(act, dec_low, preferred_element_type=F32).astype(BF)
    decoded = scatter(term_a.reshape(NS, NX, NC, rows, half), ends, near, core)

    def finish(total, own, bias):
        total = total + bias[None, None, :]
        return total[0].astype(BF), ((total - own.astype(F32)) * cot_scale).astype(BF)

    recon_b, cot_chip = finish(decoded[1], tok_chip, dec_bias[half:])
    recon_a, cot_line = finish(decoded[0], tok_line, dec_bias[:half])
    cot_a, cot_b, slope = gather(cot_line, cot_chip, core, slope)

    over_cols = (((1,), (1,)), ((), ()))
    over_rows = (((0,), (0,)), ((), ()))

    def product(left, right, dims):
        return lax.dot_general(left, right, dims, preferred_element_type=F32)

    def pair_sum(left, right):
        return product(left[0], right[0], over_rows) + product(left[1], right[1], over_rows)

    dec_b = split_core(pair_sum(act_b, cot_b).astype(BF), core)
    dec_a = split_core(product(act, cot_a, over_rows).astype(BF), core)
    dec_a, dec_b, cot_a, cot_b = tie(dec_a, dec_b, cot_a, cot_b)
    came_b, came_a = core_swap(dec_b[1]), core_swap(dec_a[1])
    grad = product(cot_a, dec_low, over_cols) + as_a(
        *[product(part, dec_high, over_cols) for part in cot_b]
    )
    came_a, came_b, grad = tie(came_a, came_b, grad)
    dec_chip = from_here(add(dec_a[0], came_a), add(dec_b[0], came_b))
    dec_far = y_first(dec_chip)
    pre_grad = (grad * slope).astype(BF)
    pre_grad, pre_grad_b = tie(pre_grad, as_b(pre_grad))
    enc_b = split_core(pair_sum(pre_grad_b, tok_b).astype(BF), core)
    enc_a = split_core(product(pre_grad, tok_a, over_rows).astype(BF), core)
    dec_far, enc_a, enc_b = tie(dec_far, enc_a, enc_b)
    dec_both = y_second(dec_chip, *dec_far)
    came_b, came_a = core_swap(enc_b[1]), core_swap(enc_a[1])
    enc_chip = from_here(add(enc_a[0], came_a), add(enc_b[0], came_b))
    enc_far = y_first(enc_chip)
    enc_far, dec_both = tie(enc_far, dec_both)
    enc_both = y_second(enc_chip, *enc_far)
    dec_grad = y_total(dec_chip, *dec_both)
    enc_grad = y_total(enc_chip, *enc_both).T
    return (jnp.concatenate([recon_a, recon_b], axis=1), enc_grad, dec_grad)


def solution(mesh):
    placed = (
        P(("tok", "lat"), None),
        P(None, "lat"),
        P("lat"),
        P("lat", None),
        P(),
        P("tok", None),
    )
    return jax.shard_map(
        shards,
        mesh=mesh,
        in_specs=placed,
        out_specs=(P(("tok", "lat"), None), P("tok", "lat"), P("lat", "tok")),
        check_vma=False,
    )
```

```python
import math

import jax
import jax.numpy as jnp
from jax import lax
from jax.sharding import PartitionSpec as P

LB = 256
NX, NZ, NY, NC = 4, 8, 4, 2
NS = NZ // 2
BF = jnp.bfloat16
F32 = jnp.float32
BOTH = ("tok", "lat")


def index_of(y, c, x, z):
    return (((y % NY) * NC + c) * NX + x % NX) * NZ + z % NZ


def everywhere(cores=(0, 1)):
    return [
        (y, c, x, z) for y in range(NY) for c in cores for x in range(NX) for z in range(NZ)
    ]


def x_shift(value, step):
    pairs = [(index_of(y, c, x, z), index_of(y, c, x + step, z)) for y, c, x, z in everywhere()]
    return lax.ppermute(value, BOTH, pairs)


def y_shift(value, step):
    pairs = [(index_of(y, c, x, z), index_of(y + step, c, x, z)) for y, c, x, z in everywhere()]
    return lax.ppermute(value, BOTH, pairs)


def z_turn(value, step, cores=(0, 1)):
    pairs = [
        (index_of(y, c, x, z), index_of(y, c, x, z + (step if c == 0 else -step)))
        for y, c, x, z in everywhere(cores)
    ]
    return lax.ppermute(value, BOTH, pairs)


def core_swap(value):
    pairs = [(index_of(y, c, x, z), index_of(y, 1 - c, x, z)) for y, c, x, z in everywhere()]
    return lax.ppermute(value, BOTH, pairs)


def add(left, right):
    return (left.astype(F32) + right.astype(F32)).astype(BF)


def tie(*values):
    return lax.optimization_barrier(values)


def gather_head(own_a, own_b):
    chip_b = jnp.stack([own_b, core_swap(own_b)], axis=0)
    line = jnp.stack([own_a] + [x_shift(own_a, -k) for k in range(1, NX)], axis=0)
    return line, chip_b


def gather(line, chip_b, core, extra):
    first = core == 0
    width = line.shape[2]
    one, two = z_turn(chip_b, -1), z_turn(chip_b, -2)
    chip_a = jnp.stack([line, core_swap(line)], axis=1)
    step_1 = z_turn(chip_a, -1)
    near = jnp.stack([one, two], axis=0)
    far = z_turn(near, -2)
    near_1, near_3 = x_shift(near, -1), x_shift(near, 1)
    ends = jnp.stack([jnp.where(first, chip_b, far[1]), far[0]], axis=0)
    ends, step_1, near_1, near_3, extra = tie(ends, step_1, near_1, near_3, extra)
    step_2 = z_turn(step_1, -1)
    ends_1, ends_3 = x_shift(ends, -1), x_shift(ends, 1)
    near_2 = x_shift(near_1, -1)
    step_2, ends_1, ends_3 = tie(step_2, ends_1, ends_3)
    step_3 = z_turn(step_2, -1)
    ends_2 = x_shift(ends_3, 1)
    step_4 = z_turn(step_3, -1, cores=(1,))
    whole_a = jnp.stack([jnp.where(first, chip_a, step_4), step_3, step_1, step_2], axis=0)
    ends_b = jnp.stack([ends, ends_1, ends_2, ends_3], axis=0)
    near_b = jnp.stack([near, near_1, near_2, near_3], axis=0)
    return whole_a.reshape(-1, width), (ends_b.reshape(-1, width), near_b.reshape(-1, width)), extra


def scatter(terms_a, ends, near, core):
    first = core == 0
    ends_up, ends_far = x_shift(ends[1], 1), x_shift(ends[2], -1)
    step = z_turn(terms_a[0], 1, cores=(1,))
    ends_up, ends_far, step = tie(ends_up, ends_far, step)
    step, ends_far = tie(add(terms_a[1], step), ends_far)
    step = z_turn(step, 1)
    ends_down = x_shift(add(ends[3], ends_far), -1)
    near_far = x_shift(near[2], 1)
    ends_down, near_far, step = tie(ends_down, near_far, step)
    step, ends_down, near_far = tie(add(terms_a[3], step), ends_down, near_far)
    step = z_turn(step, 1)
    ends_sum = (ends[0].astype(F32) + ends_up.astype(F32) + ends_down.astype(F32)).astype(BF)
    far = z_turn(ends_sum, 2)
    near_up, near_down = x_shift(add(near[1], near_far), 1), x_shift(near[3], -1)
    far, near_up, near_down, step = tie(far, near_up, near_down, step)
    step, far, near_up, near_down = tie(add(terms_a[2], step), far, near_up, near_down)
    step = z_turn(step, 1)
    near_sum = near[0].astype(F32) + near_up.astype(F32) + near_down.astype(F32)
    one = z_turn(add(near_sum[0], far[1]), 1)
    two = z_turn(add(near_sum[1], jnp.where(first, jnp.zeros_like(far[0]), far[0])), 2)

    chip_a = step.astype(F32) + jnp.where(first, terms_a[0].astype(F32), 0.0)
    chip_b = one.astype(F32) + two.astype(F32) + jnp.where(first, ends_sum[0].astype(F32), 0.0)
    line = (chip_a[:, 0] + core_swap(chip_a[:, 1].astype(BF)).astype(F32)).astype(BF)
    came_b = core_swap(chip_b.astype(BF))
    total_b = chip_b + came_b[::-1].astype(F32)
    total_a = line.astype(F32)
    for k in range(1, NX):
        total_a = total_a + jnp.roll(x_shift(line, -k), k, axis=0).astype(F32)
    return total_a, total_b


def split_core(part, core):
    blocks = NY // 2
    block = part.shape[1] // (blocks * NC)

    def take(c):
        pieces = [
            lax.dynamic_slice_in_dim(part, (j * NC + c) * block, block, 1) for j in range(blocks)
        ]
        return jnp.stack(pieces, axis=0)

    return take(core), take(1 - core)


def from_here(low, high):
    whole = jnp.concatenate([low, high], axis=0)
    y_here = lax.axis_index("tok") // NC
    return jnp.stack(
        [lax.dynamic_index_in_dim(whole, (y_here + k) % NY, 0, keepdims=False) for k in range(NY)],
        axis=0,
    )


def y_first(chip):
    half = chip.shape[1] // 2
    return y_shift(chip[2, :half], 1), y_shift(chip[2, half:], -1)


def y_second(chip, far_up, far_down):
    half = chip.shape[1] // 2
    up = jnp.concatenate([add(chip[1, :half], far_up), chip[1, half:]], axis=0)
    down = jnp.concatenate([chip[3, :half], add(chip[3, half:], far_down)], axis=0)
    return y_shift(up, 1), y_shift(down, -1)


def y_total(chip, up, down):
    return chip[0].astype(F32) + up.astype(F32) + down.astype(F32)


def shards(tokens, enc_weight, enc_bias, dec_weight, dec_bias, active_blocks):
    rows, depth = tokens.shape
    latent_width = enc_weight.shape[1]
    half = depth // 2
    here = NS * NX * NC * rows
    cot_scale = 1.0 / math.sqrt(rows * NX * NZ * NY * NC)
    owner = lax.axis_index("lat")
    core = lax.axis_index("tok") % NC
    x_here = owner // NZ

    def swapped(part, outer, inner):
        shaped = part.reshape(outer, inner, NC * rows, -1)
        return jnp.swapaxes(shaped, 0, 1).reshape(part.shape)

    def as_a(ends, near):
        return jnp.concatenate([swapped(ends, NX, 2), swapped(near, NX, 2)], axis=0)

    def as_b(whole):
        return swapped(whole[: here // 2], 2, NX), swapped(whole[here // 2 :], 2, NX)

    tok_line, tok_chip = gather_head(tokens[:, :half], tokens[:, half:])
    tok_a, tok_b, lists = gather(tok_line, tok_chip, core, active_blocks)

    lists = jnp.stack([lists, core_swap(lists)], axis=0)
    hits = jnp.any(lists == owner, axis=2).astype(F32)
    blocks = active_blocks.shape[0]
    x_block = ((x_here + jnp.arange(NX)) % NX) // (NX // blocks)
    gate = sum(jnp.where(x_block[:, None] == b, hits[None, :, b], 0.0) for b in range(blocks))
    gate = jnp.broadcast_to(gate[None, :, :, None], (NS, NX, NC, rows)).reshape(here, 1)

    enc_low, enc_high = enc_weight[:half], enc_weight[half:]
    dec_low, dec_high = dec_weight[:, :half], dec_weight[:, half:]
    pre_b = [jnp.dot(part, enc_high, preferred_element_type=F32) for part in tok_b]
    pre_act = jnp.dot(tok_a, enc_low, preferred_element_type=F32)
    pre_act = pre_act + as_a(*pre_b) + enc_bias[None, :]
    act = (jax.nn.silu(pre_act) * gate).astype(BF)
    act_b = as_b(act)
    sigma = jax.nn.sigmoid(pre_act)
    slope = sigma * (1.0 + pre_act * (1.0 - sigma)) * gate
    act, act_b, slope = tie(act, act_b, slope)

    ends, near = [
        jnp.dot(part, dec_high, preferred_element_type=F32)
        .astype(BF)
        .reshape(NX, 2, NC, rows, half)
        for part in act_b
    ]
    term_a = jnp.dot(act, dec_low, preferred_element_type=F32).astype(BF)
    decoded = scatter(term_a.reshape(NS, NX, NC, rows, half), ends, near, core)

    def finish(total, own, bias):
        total = total + bias[None, None, :]
        return total[0].astype(BF), ((total - own.astype(F32)) * cot_scale).astype(BF)

    recon_b, cot_chip = finish(decoded[1], tok_chip, dec_bias[half:])
    recon_a, cot_line = finish(decoded[0], tok_line, dec_bias[:half])
    cot_a, cot_b, slope = gather(cot_line, cot_chip, core, slope)

    over_cols = (((1,), (1,)), ((), ()))
    over_rows = (((0,), (0,)), ((), ()))

    def product(left, right, dims):
        return lax.dot_general(left, right, dims, preferred_element_type=F32)

    def pair_sum(left, right):
        return product(left[0], right[0], over_rows) + product(left[1], right[1], over_rows)

    dec_b = split_core(pair_sum(act_b, cot_b).astype(BF), core)
    dec_a = split_core(product(act, cot_a, over_rows).astype(BF), core)
    dec_a, cot_a, cot_b = tie(dec_a, cot_a, cot_b)
    came_b, came_a = core_swap(dec_b[1]), core_swap(dec_a[1])
    grad = product(cot_a, dec_low, over_cols) + as_a(
        *[product(part, dec_high, over_cols) for part in cot_b]
    )
    came_a, came_b, grad = tie(came_a, came_b, grad)
    dec_chip = from_here(add(dec_a[0], came_a), add(dec_b[0], came_b))
    dec_far = y_first(dec_chip)
    pre_grad = (grad * slope).astype(BF)
    pre_grad, pre_grad_b = tie(pre_grad, as_b(pre_grad))
    enc_b = split_core(pair_sum(pre_grad_b, tok_b).astype(BF), core)
    enc_a = split_core(product(pre_grad, tok_a, over_rows).astype(BF), core)
    dec_far, enc_a, enc_b = tie(dec_far, enc_a, enc_b)
    dec_both = y_second(dec_chip, *dec_far)
    came_b, came_a = core_swap(enc_b[1]), core_swap(enc_a[1])
    enc_chip = from_here(add(enc_a[0], came_a), add(enc_b[0], came_b))
    enc_far = y_first(enc_chip)
    enc_far, dec_both = tie(enc_far, dec_both)
    enc_both = y_second(enc_chip, *enc_far)
    dec_grad = y_total(dec_chip, *dec_both)
    enc_grad = y_total(enc_chip, *enc_both).T
    return (jnp.concatenate([recon_a, recon_b], axis=1), enc_grad, dec_grad)


def solution(mesh):
    placed = (
        P(("tok", "lat"), None),
        P(None, "lat"),
        P("lat"),
        P("lat", None),
        P(),
        P("tok", None),
    )
    return jax.shard_map(
        shards,
        mesh=mesh,
        in_specs=placed,
        out_specs=(P(("tok", "lat"), None), P("tok", "lat"), P("lat", "tok")),
        check_vma=False,
    )
```
